32 devices in a mesh: dp: 4 (over z), ctx: 2 (over y), tensor: 4 (over x, core).
Axes of the slice: x: 2, y: 2, z: 4, core: 2. Of those that a mesh axis runs over, the one named last changes fastest.
Arguments:
- tokens: bfloat16 [8, 2048, 768], P('dp', ('ctx', 'tensor')), may hold values from -6 to 6
- cotangent: bfloat16 [8, 2048, 768], P('dp', 'ctx'), may hold values from -6 to 6
- stretch_order: int32 [8, 4], P('dp'), may hold values from 0 to 3, each once within a row
- attn_gain: bfloat16 [768], P(('dp', 'ctx')), may hold values from 0.5 to 1.5
- attn_shift: bfloat16 [768], P(('dp', 'ctx')), may hold values from -2 to 2
- heads_weight: bfloat16 [3, 768, 768], P(None, ('dp', 'ctx'), 'tensor'), may hold values from -0.21875 to 0.21875
- heads_bias: bfloat16 [2, 768], P(None, ('dp', 'ctx')), may hold values from -0.59765625 to 0.59765625
- merge_weight: bfloat16 [768, 768], P('tensor', ('dp', 'ctx')), may hold values from -1.75 to 1.75
- merge_bias: bfloat16 [768], P(('dp', 'ctx')), may hold values from -3 to 3
- feed_gain: bfloat16 [768], P(('dp', 'ctx')), may hold values from 0.5 to 1.5
- feed_shift: bfloat16 [768], P(('dp', 'ctx')), may hold values from -2 to 2
- up_weight: bfloat16 [768, 3072], P(('dp', 'ctx'), 'tensor'), may hold values from -0.21875 to 0.21875
- up_bias: bfloat16 [3072], P(('dp', 'ctx')), may hold values from -2 to 2
- down_weight: bfloat16 [3072, 768], P('tensor', ('dp', 'ctx')), may hold values from -0.109375 to 0.109375
- down_bias: bfloat16 [768], P(('dp', 'ctx')), may hold values from -3 to 3
Outputs:
- block_out: bfloat16 [8, 2048, 768], P('dp', ('ctx', 'tensor'))
- tokens_grad: float32 [8, 2048, 768], P('dp', ('ctx', 'tensor'))
- attn_gain_grad: float32 [768], P(('dp', 'ctx'))
- attn_shift_grad: float32 [768], P(('dp', 'ctx'))
- heads_weight_grad: float32 [3, 768, 768], P(None, ('dp', 'ctx'), 'tensor')
- heads_bias_grad: float32 [2, 768], P(None, ('dp', 'ctx'))
- merge_weight_grad: float32 [768, 768], P('tensor', ('dp', 'ctx'))
- merge_bias_grad: float32 [768], P(('dp', 'ctx'))
- feed_gain_grad: float32 [768], P(('dp', 'ctx'))
- feed_shift_grad: float32 [768], P(('dp', 'ctx'))
- up_weight_grad: float32 [768, 3072], P(('dp', 'ctx'), 'tensor')
- up_bias_grad: float32 [3072], P(('dp', 'ctx'))
- down_weight_grad: float32 [3072, 768], P('tensor', ('dp', 'ctx'))
- down_bias_grad: float32 [768], P(('dp', 'ctx'))
The draws below stay inside these ranges and needn't reach their ends.
Inputs may be any that keep to these rules, and one draw needn't show every extreme that they name: Each row of stretch_order is a permutation of the 4 stretch numbers; the tokens of stored stretch k of sequence s stand at positions stretch_order[s, k] * 512 and onward.
All inputs are finite; a program needn't handle non-finite values.
Results may differ from the reference program's by a relative error of at most 0.023.
Values may be sent and summed in bfloat16 or wider, within the bound.
No kernel may reach another device: no remote copies, remote signals or barrier semaphores. Data moves between devices by JAX's collectives and lax.ppermute only.
A program may use at most 192 MiB of HBM per device.

```python
import jax
import jax.numpy as jnp
from jax import lax

D = 768
HEADS = 12
HEAD_DIM = 64
FF = 3072
SEQ_LEN = 2048
SEQS = 8
STRETCH = 512
N_CTX = 2


def levels(rng, extent, shards, least, top_value):
    def one(dim, shards_of):
        heights = jax.random.uniform(jax.random.fold_in(jax.random.fold_in(rng, 6), dim), (shards_of,), jnp.float32, least / len(shards), top_value / len(shards))
        return jnp.repeat(jnp.exp(heights), extent[dim] // shards_of).reshape((-1,) + (1,) * (len(extent) - dim - 1))

    level = one(*shards[0])
    for cut in shards[1:]:
        level = level * one(*cut)
    return level


def gaussian(key, extent, scale, most, split=(), kind=jnp.bfloat16):
    entries = jax.random.normal(key, extent, jnp.float32) * scale
    if len(split) > 0:
        entries = levels(key, extent, split, -0.22, 0.18) * entries
    return jnp.clip(entries, min=-most, max=most).astype(kind)


def setup_inputs(seed: int = 0) -> dict:
    arg_keys = jax.random.split(jax.random.key(seed), 16)
    tokens = gaussian(arg_keys[0], (SEQS, SEQ_LEN, D), 1.0, 6.0, ((0, 4), (1, 8)))
    cotangent = gaussian(arg_keys[1], (SEQS, SEQ_LEN, D), 1.0, 6.0, ((0, 4), (1, 2)))
    stretch_order = jax.vmap(lambda own: jax.random.permutation(own, 2 * N_CTX))(jax.random.split(arg_keys[2], SEQS)).reshape((SEQS, 2 * N_CTX)).astype(jnp.int32)
    attn_gain = jnp.clip(1.0 + 0.1 * jax.random.normal(arg_keys[3], (D,), jnp.float32), 0.5, 1.5).astype(jnp.bfloat16)
    attn_shift = gaussian(arg_keys[4], (D,), 0.3, 2.0, ((0, 8),))
    heads_weight = gaussian(arg_keys[5], (3, D, D), D ** -0.5, 0.21875, ((1, 8), (2, 4)))
    heads_bias = gaussian(arg_keys[6], (2, D), 0.1, 0.59765625, ((1, 8),))
    merge_weight = gaussian(arg_keys[7], (D, D), (max(4, D // 64)) ** -0.5, 1.75, ((0, 4), (1, 8)))
    merge_bias = gaussian(arg_keys[8], (D,), 0.5, 3.0, ((0, 8),))
    feed_gain = jnp.clip(1.0 + 0.1 * jax.random.normal(arg_keys[9], (D,), jnp.float32), 0.5, 1.5).astype(jnp.bfloat16)
    feed_shift = gaussian(arg_keys[10], (D,), 0.3, 2.0, ((0, 8),))
    up_weight = gaussian(arg_keys[11], (D, FF), D ** -0.5, 0.21875, ((0, 8), (1, 4)))
    up_bias = gaussian(arg_keys[12], (FF,), 0.3, 2.0, ((0, 8),))
    down_weight = gaussian(arg_keys[13], (FF, D), FF ** -0.5, 0.109375, ((0, 4), (1, 8)))
    down_bias = gaussian(arg_keys[14], (D,), 0.5, 3.0, ((0, 8),))
    return dict(tokens=tokens, cotangent=cotangent, stretch_order=stretch_order, attn_gain=attn_gain, attn_shift=attn_shift, heads_weight=heads_weight, heads_bias=heads_bias, merge_weight=merge_weight, merge_bias=merge_bias, feed_gain=feed_gain, feed_shift=feed_shift, up_weight=up_weight, up_bias=up_bias, down_weight=down_weight, down_bias=down_bias)


EPS = 1e-05
GELU_C = 0.7978845608028654
NEG = -1e+30
HIGH = lax.Precision.HIGHEST

@jax.custom_vjp
def low(v):
    return lax.optimization_barrier(v.astype(jnp.bfloat16)).astype(jnp.float32)

@jax.custom_vjp
def low_back(v):
    return v

def low_keep(v):
    return (low(v), None)

def low_pass(kept, grad):
    return (grad,)

def back_keep(v):
    return (v, None)

def back_low(kept, grad):
    return (low(grad),)
low.defvjp(low_keep, low_pass)
low_back.defvjp(back_keep, back_low)

def layer_norm(rows):
    centred = rows - lax.optimization_barrier(jnp.mean(rows, axis=-1, keepdims=True))
    return centred * lax.rsqrt(lax.optimization_barrier(jnp.mean(centred * centred, axis=-1, keepdims=True)) + EPS)

def smooth_gelu(values):
    return 0.5 * values * (1.0 + jnp.tanh(GELU_C * (values + 0.044715 * values * values * values)))

def matmul(left, right):
    return jnp.dot(left, right, precision=HIGH)

def forward(params, rows, positions):
    gain_one, shift_one, w_heads, b_heads, w_merge, b_merge, gain_two, shift_two, w_up, b_up, w_down, b_down = params
    normed = low(layer_norm(rows) * gain_one + shift_one)
    queries = low(low_back(matmul(normed, w_heads[0])) + b_heads[0])
    keys_all = low(low_back(matmul(normed, w_heads[1])))
    values = low(low_back(matmul(normed, w_heads[2])) + b_heads[1])
    allowed = positions[None, :] <= positions[:, None]

    def split_heads(matrix):
        return jnp.transpose(matrix.reshape(SEQ_LEN, HEADS, HEAD_DIM), (1, 0, 2))

    def head_fn(head_item):
        query_head, key_head, value_head = head_item
        scores = low_back(matmul(query_head, key_head.T)) * HEAD_DIM ** (-0.5)
        scores = jnp.where(allowed, scores, NEG)
        row_max = lax.optimization_barrier(jnp.max(scores, axis=-1, keepdims=True))
        log_total = row_max + jnp.log(lax.optimization_barrier(jnp.sum(jnp.exp(scores - row_max), axis=-1, keepdims=True)))
        probs = jnp.exp(scores - log_total)
        return matmul(low(probs), value_head)
    attended = lax.map(jax.checkpoint(head_fn), (split_heads(queries), split_heads(keys_all), split_heads(values)))
    joined = low(low_back(jnp.transpose(attended, (1, 0, 2)).reshape(SEQ_LEN, D)))
    resid = rows + low_back(matmul(joined, w_merge)) + b_merge
    normed_two = low(layer_norm(resid) * gain_two + shift_two)
    pre_act = low_back(matmul(normed_two, w_up)) + b_up
    activ = low(smooth_gelu(pre_act))
    return resid + low_back(matmul(activ, w_down)) + b_down

def reference(tokens, cotangent, stretch_order, attn_gain, attn_shift, heads_weight, heads_bias, merge_weight, merge_bias, feed_gain, feed_shift, up_weight, up_bias, down_weight, down_bias):
    params = tuple((item.astype(jnp.float32) for item in (attn_gain, attn_shift, heads_weight, heads_bias, merge_weight, merge_bias, feed_gain, feed_shift, up_weight, up_bias, down_weight, down_bias)))
    row_index = jnp.arange(SEQ_LEN, dtype=jnp.int32)

    def one_sequence(running, seq_item):
        seq_rows, seq_grad, seq_order = seq_item
        positions = seq_order[row_index // STRETCH] * STRETCH + row_index % STRETCH

        def run_layer(param_set, rows):
            return forward(param_set, rows, positions)
        outputs, pullback = jax.vjp(run_layer, params, seq_rows.astype(jnp.float32))
        param_grads, row_grads = pullback(seq_grad.astype(jnp.float32))
        running = jax.tree.map(jnp.add, running, param_grads)
        return (running, (outputs.astype(jnp.bfloat16), row_grads))
    zeros_start = jax.tree.map(jnp.zeros_like, params)
    grads, (block_out, tokens_grad) = lax.scan(one_sequence, zeros_start, (tokens, cotangent, stretch_order))
    return (block_out, tokens_grad, grads[0], grads[1], grads[2], grads[3], grads[4], grads[5], grads[6], grads[7], grads[8], grads[9], grads[10], grads[11])
```

```python
import functools

import jax
import jax.numpy as jnp
from jax import lax
from jax.experimental import pallas as pl
from jax.experimental.pallas import tpu as pltpu
from jax.sharding import PartitionSpec as P

HEAD_DIM = 64
EPS = 1e-05
GELU_C = 0.7978845608028654
NEG = -1e30
TILE = 256
F32 = jnp.float32
BF16 = jnp.bfloat16


def layer_stats(rows):
    centred = rows - jnp.mean(rows, axis=-1, keepdims=True)
    inv_std = lax.rsqrt(jnp.mean(centred * centred, axis=-1, keepdims=True) + EPS)
    return (centred * inv_std, inv_std)


def norm_back(grad_out, normed, inv_std, gain):
    scaled = grad_out * gain
    return inv_std * (
        scaled
        - jnp.mean(scaled, axis=-1, keepdims=True)
        - normed * jnp.mean(scaled * normed, axis=-1, keepdims=True)
    )


def dot(left, right, dims=((1,), (0,))):
    return lax.dot_general(left, right, (dims, ((), ())), preferred_element_type=F32)


def causal_tile(size):
    key_row = lax.broadcasted_iota(jnp.int32, (size, size), 0)
    query_col = lax.broadcasted_iota(jnp.int32, (size, size), 1)
    return key_row <= query_col


def attend_kernel(
    pieces, heads, starts, qkv, q_pos, k_pos, v_pos, out_t, lse, out, q_t, v_t, k_h, o_nat
):
    seq = pl.program_id(0)
    length, width = q_pos.shape
    rows = length // pieces
    blocks = length // TILE
    for p in range(pieces):
        first = pl.multiple_of(starts[seq * pieces + p], rows)
        part = qkv[pl.ds(first, rows), :]
        here = slice(p * rows, (p + 1) * rows)
        q_pos[here, :] = part[:, :width] * jnp.asarray(HEAD_DIM ** (-0.5), BF16)
        k_pos[here, :] = part[:, width : 2 * width]
        v_pos[here, :] = part[:, 2 * width :]
    for b in range(blocks):
        here = slice(b * TILE, (b + 1) * TILE)
        q_t[:, here] = q_pos[here, :].T
        v_t[:, here] = v_pos[here, :].T
        key = k_pos[here, :]
        for h in range(heads):
            k_h[h, here, :] = key[:, h * HEAD_DIM : (h + 1) * HEAD_DIM]
    allowed = causal_tile(TILE)

    def one_head(h, unused):
        hs = pl.ds(pl.multiple_of(h * HEAD_DIM, HEAD_DIM), HEAD_DIM)
        for i in range(blocks):
            here = slice(i * TILE, (i + 1) * TILE)
            query = q_t[hs, here]
            diag = jnp.where(allowed, dot(k_h[h, here, :], query), NEG)
            top = jnp.max(diag, axis=0, keepdims=True)
            if i > 0:
                past = dot(k_h[h, : i * TILE, :], query)
                top = jnp.maximum(top, jnp.max(past, axis=0, keepdims=True))
            diag = jnp.exp(diag - top)
            total = jnp.sum(diag, axis=0, keepdims=True)
            mixed = dot(v_t[hs, here], diag.astype(BF16))
            if i > 0:
                past = jnp.exp(past - top)
                total += jnp.sum(past, axis=0, keepdims=True)
                mixed += dot(v_t[hs, : i * TILE], past.astype(BF16))
            out_t[hs, here] = mixed / total
            lse[h, :, here] = top + jnp.log(total)
        return unused

    lax.fori_loop(0, heads, one_head, 0)
    for b in range(blocks):
        here = slice(b * TILE, (b + 1) * TILE)
        o_nat[here, :] = out_t[:, here].T.astype(BF16)
    for p in range(pieces):
        first = pl.multiple_of(starts[seq * pieces + p], rows)
        out[pl.ds(first, rows), :] = o_nat[p * rows : (p + 1) * rows, :]


def attend(starts, qkv, seqs, pieces):
    total, triple = qkv.shape
    width = triple // 3
    heads = width // HEAD_DIM
    length = total // seqs
    nat = jax.ShapeDtypeStruct((seqs, length, width), BF16)
    nat_spec = pl.BlockSpec((None, length, width), lambda s, t: (s, 0, 0))
    pairs = heads * length * (length + TILE) // 2 * seqs
    return pl.pallas_call(
        functools.partial(attend_kernel, pieces, heads),
        grid_spec=pltpu.PrefetchScalarGridSpec(
            num_scalar_prefetch=1,
            grid=(seqs,),
            in_specs=[pl.BlockSpec((total, triple), lambda s, t: (0, 0))],
            out_specs=[
                nat_spec,
                nat_spec,
                nat_spec,
                pl.BlockSpec((None, width, length), lambda s, t: (s, 0, 0)),
                pl.BlockSpec((None, heads, 1, length), lambda s, t: (s, 0, 0, 0)),
                pl.BlockSpec((total, width), lambda s, t: (0, 0)),
            ],
            scratch_shapes=[
                pltpu.VMEM((width, length), BF16),
                pltpu.VMEM((width, length), BF16),
                pltpu.VMEM((heads, length, HEAD_DIM), BF16),
                pltpu.VMEM((length, width), BF16),
            ],
        ),
        out_shape=[
            nat,
            nat,
            nat,
            jax.ShapeDtypeStruct((seqs, width, length), F32),
            jax.ShapeDtypeStruct((seqs, heads, 1, length), F32),
            jax.ShapeDtypeStruct((total, width), BF16),
        ],
        compiler_params=pltpu.CompilerParams(vmem_limit_bytes=56 * 2**20),
        cost_estimate=pl.CostEstimate(
            flops=16 * HEAD_DIM * pairs, bytes_accessed=12 * total * triple, transcendentals=pairs
        ),
        name="attend",
    )(starts, qkv)


def attend_back_kernel(
    pieces,
    heads,
    starts,
    grad_out,
    q_pos,
    k_pos,
    v_pos,
    out_t,
    lse,
    grad_qkv,
    bias_sum,
    do_nat,
    q_t,
    k_t,
    do_t,
    q_h,
    k_h,
    v_h,
    do_h,
    row_dot,
    dq_t,
    dk_h,
    dv_h,
    g_nat,
):
    seq = pl.program_id(0)
    length, width = q_pos.shape
    rows = length // pieces
    blocks = length // TILE
    for p in range(pieces):
        first = pl.multiple_of(starts[seq * pieces + p], rows)
        do_nat[p * rows : (p + 1) * rows, :] = grad_out[pl.ds(first, rows), :]
    for b in range(blocks):
        here = slice(b * TILE, (b + 1) * TILE)
        query, key, value, grad = q_pos[here, :], k_pos[here, :], v_pos[here, :], do_nat[here, :]
        q_t[:, here] = query.T
        k_t[:, here] = key.T
        grad_t = grad.T
        do_t[:, here] = grad_t
        product = grad_t.astype(F32) * out_t[:, here]
        for h in range(heads):
            cols = slice(h * HEAD_DIM, (h + 1) * HEAD_DIM)
            q_h[h, here, :] = query[:, cols]
            k_h[h, here, :] = key[:, cols]
            v_h[h, here, :] = value[:, cols]
            do_h[h, here, :] = grad[:, cols]
            row_dot[h, :, here] = jnp.sum(product[cols, :], axis=0, keepdims=True)
    allowed = causal_tile(TILE)

    def one_head(h, unused):
        hs = pl.ds(pl.multiple_of(h * HEAD_DIM, HEAD_DIM), HEAD_DIM)
        for j in range(blocks):
            here = slice(j * TILE, (j + 1) * TILE)
            key, value = k_h[h, here, :], v_h[h, here, :]
            key_t = k_t[hs, here]
            scores = jnp.where(allowed, dot(key, q_t[hs, here]), NEG)
            probs = jnp.exp(scores - lse[h, :, here])
            slope = probs * (dot(value, do_t[hs, here]) - row_dot[h, :, here])
            slope_low = slope.astype(BF16)
            grad_v = dot(probs.astype(BF16), do_h[h, here, :])
            grad_k = dot(slope_low, q_h[h, here, :])
            add = dot(key_t, slope_low)
            dq_t[hs, here] = add if j == 0 else dq_t[hs, here] + add
            if j < blocks - 1:
                later = slice((j + 1) * TILE, length)
                probs = jnp.exp(dot(key, q_t[hs, later]) - lse[h, :, later])
                slope = probs * (dot(value, do_t[hs, later]) - row_dot[h, :, later])
                slope_low = slope.astype(BF16)
                grad_v += dot(probs.astype(BF16), do_h[h, later, :])
                grad_k += dot(slope_low, q_h[h, later, :])
                add = dot(key_t, slope_low)
                dq_t[hs, later] = add if j == 0 else dq_t[hs, later] + add
            dk_h[h, here, :] = grad_k
            dv_h[h, here, :] = grad_v
        return unused

    lax.fori_loop(0, heads, one_head, 0)
    sum_q = jnp.zeros((1, width), F32)
    sum_v = jnp.zeros((1, width), F32)
    for b in range(blocks):
        here = slice(b * TILE, (b + 1) * TILE)
        grad_q = dq_t[:, here].T * (HEAD_DIM ** (-0.5))
        grad_k = jnp.concatenate([dk_h[h, here, :] for h in range(heads)], axis=1)
        grad_v = jnp.concatenate([dv_h[h, here, :] for h in range(heads)], axis=1)
        sum_q += jnp.sum(grad_q, axis=0, keepdims=True)
        sum_v += jnp.sum(grad_v, axis=0, keepdims=True)
        g_nat[here, :] = jnp.concatenate([grad_q, grad_k, grad_v], axis=1).astype(BF16)
    for p in range(pieces):
        first = pl.multiple_of(starts[seq * pieces + p], rows)
        grad_qkv[pl.ds(first, rows), :] = g_nat[p * rows : (p + 1) * rows, :]
    bias_sum[...] = jnp.concatenate([sum_q, sum_v], axis=0)


def attend_back(starts, grad_out, q_pos, k_pos, v_pos, out_t, lse, pieces):
    total, width = grad_out.shape
    seqs, length, unused = q_pos.shape
    heads = width // HEAD_DIM
    nat_spec = pl.BlockSpec((None, length, width), lambda s, t: (s, 0, 0))
    pairs = heads * length * (length + TILE) // 2 * seqs
    per_head = pltpu.VMEM((heads, length, HEAD_DIM), BF16)
    across = pltpu.VMEM((width, length), BF16)
    return pl.pallas_call(
        functools.partial(attend_back_kernel, pieces, heads),
        grid_spec=pltpu.PrefetchScalarGridSpec(
            num_scalar_prefetch=1,
            grid=(seqs,),
            in_specs=[
                pl.BlockSpec((total, width), lambda s, t: (0, 0)),
                nat_spec,
                nat_spec,
                nat_spec,
                pl.BlockSpec((None, width, length), lambda s, t: (s, 0, 0)),
                pl.BlockSpec((None, heads, 1, length), lambda s, t: (s, 0, 0, 0)),
            ],
            out_specs=[
                pl.BlockSpec((total, 3 * width), lambda s, t: (0, 0)),
                pl.BlockSpec((None, 2, width), lambda s, t: (s, 0, 0)),
            ],
            scratch_shapes=[
                pltpu.VMEM((length, width), BF16),
                across,
                across,
                across,
                per_head,
                per_head,
                per_head,
                per_head,
                pltpu.VMEM((heads, 1, length), F32),
                pltpu.VMEM((width, length), F32),
                pltpu.VMEM((heads, length, HEAD_DIM), F32),
                pltpu.VMEM((heads, length, HEAD_DIM), F32),
                pltpu.VMEM((length, 3 * width), BF16),
            ],
        ),
        out_shape=[
            jax.ShapeDtypeStruct((total, 3 * width), BF16),
            jax.ShapeDtypeStruct((seqs, 2, width), F32),
        ],
        compiler_params=pltpu.CompilerParams(vmem_limit_bytes=56 * 2**20),
        cost_estimate=pl.CostEstimate(
            flops=40 * HEAD_DIM * pairs, bytes_accessed=20 * total * width, transcendentals=pairs
        ),
        name="attend_back",
    )(starts, grad_out, q_pos, k_pos, v_pos, out_t, lse)


def swap_tensor(block, bit):
    size = lax.axis_size("tensor")
    return lax.ppermute(block, "tensor", [(i, i ^ bit) for i in range(size)])


def rotate(block, axis, distance):
    size = lax.axis_size(axis)
    return lax.ppermute(block, axis, [(i, (i + distance) % size) for i in range(size)])


def tensor_bits():
    return [1 << b for b in range(lax.axis_size("tensor").bit_length() - 1)]


def gather_tensor(own):
    for bit in reversed(tensor_bits()):
        own = jnp.concatenate([own, swap_tensor(own, bit)], axis=0)
    return own


def scatter_tensor(rows, weight_t):
    parts = None
    for bit in tensor_bits():
        half = rows.shape[0] // 2
        away = dot(rows[half:], weight_t)
        if parts is not None:
            away = away + sum(p[half:].astype(F32) for p in parts)
        moved = swap_tensor(away.astype(BF16), bit)
        parts = ([] if parts is None else [p[:half] for p in parts]) + [moved]
        rows = rows[:half]
    own = dot(rows, weight_t)
    return own + sum(p.astype(F32) for p in parts)


def pick(array, index):
    return lax.dynamic_index_in_dim(array, index, 0, keepdims=False)


def scatter_params(blocks):
    dp, ctx = lax.axis_size("dp"), lax.axis_size("ctx")
    dp_pos, ctx_pos = lax.axis_index("dp"), lax.axis_index("ctx")
    by_ctx = jnp.swapaxes(blocks, 0, 1)
    total = pick(by_ctx, ctx_pos).astype(F32)
    for d in range(1, ctx):
        total += rotate(pick(by_ctx, (ctx_pos + d) % ctx), "ctx", d).astype(F32)
    low = total.astype(BF16)
    result = pick(low, dp_pos).astype(F32)
    for d in range(1, dp):
        result += rotate(pick(low, (dp_pos + d) % dp), "dp", d).astype(F32)
    return result


def local(
    tokens,
    cotangent,
    stretch_order,
    attn_gain,
    attn_shift,
    heads_weight,
    heads_bias,
    merge_weight,
    merge_bias,
    feed_gain,
    feed_shift,
    up_weight,
    up_bias,
    down_weight,
    down_bias,
):
    t_size, t_pos = lax.axis_size("tensor"), lax.axis_index("tensor")
    c_size, c_pos = lax.axis_size("ctx"), lax.axis_index("ctx")
    dp_size = lax.axis_size("dp")
    owners = dp_size * c_size
    seqs_in, rows, model = tokens.shape
    seqs = seqs_in // c_size
    shard = heads_weight.shape[1]
    width = heads_weight.shape[2]
    hidden = up_weight.shape[1]
    hidden_all = hidden * t_size
    pieces = c_size * t_size
    rel = [0]
    for bit in reversed(tensor_bits()):
        rel = rel + [r ^ bit for r in rel]

    vectors = jnp.concatenate(
        [
            jnp.stack(
                [
                    attn_gain,
                    attn_shift,
                    heads_bias[0],
                    heads_bias[1],
                    merge_bias,
                    feed_gain,
                    feed_shift,
                    down_bias,
                ],
                axis=1,
            ),
            up_bias.reshape(shard, -1),
        ],
        axis=1,
    )
    first_pack = jnp.concatenate([heads_weight[0], heads_weight[1], heads_weight[2], vectors], axis=1)
    second_pack = jnp.concatenate([up_weight, down_weight.T, merge_weight.T], axis=1)
    first_all = lax.all_gather(first_pack, ("dp", "ctx"), axis=0, tiled=True)
    second_all = lax.all_gather(second_pack, ("dp", "ctx"), axis=0, tiled=True)
    w_heads = first_all[:, : 3 * width]
    vec = first_all[:, 3 * width :].astype(F32)
    vec_t = vec[:, :8].T
    gain_one, shift_one, b_query, b_value, b_merge, gain_two, shift_two, b_down = (
        vec_t[i] for i in range(8)
    )
    b_up = lax.dynamic_slice_in_dim(vec[:, 8:].reshape(-1), t_pos * hidden, hidden, 0)
    b_query = lax.dynamic_slice_in_dim(b_query, t_pos * width, width, 0)
    b_value = lax.dynamic_slice_in_dim(b_value, t_pos * width, width, 0)
    b_heads = jnp.concatenate([b_query, jnp.zeros_like(b_query), b_value])
    w_up = second_all[:, :hidden]
    w_down_t = second_all[:, hidden : 2 * hidden]
    w_merge_t = second_all[:, 2 * hidden :]

    by_owner = tokens.reshape(c_size, seqs, rows, model)
    own = [pick(by_owner, c_pos)] + [
        rotate(pick(by_owner, (c_pos - d) % c_size), "ctx", -d) for d in range(1, c_size)
    ]
    own_rows = jnp.concatenate(own, axis=0).reshape(-1, model)
    tokens_all = gather_tensor(own_rows)

    per_stretch = t_size // 2
    order = lax.dynamic_slice_in_dim(stretch_order, c_pos * seqs, seqs, 0)
    stretches = order.shape[1]
    span = jnp.arange(stretches, dtype=jnp.int32)
    inverse = jnp.sum(
        jnp.where(order[:, :, None] == span[None, None, :], span[None, :, None], 0), axis=1
    )
    stored = inverse[:, :, None]
    part = jnp.arange(per_stretch, dtype=jnp.int32)[None, None, :]
    piece_t = (stored % 2) * per_stretch + part
    piece_c = stored // 2 + 0 * part
    slot = jnp.zeros_like(piece_t)
    for index, offset in enumerate(rel):
        slot = jnp.where((piece_t ^ t_pos) == offset, index, slot)
    away = (piece_c - c_pos) % c_size
    seq_id = jnp.arange(seqs, dtype=jnp.int32)[:, None, None]
    starts = (((slot * c_size + away) * seqs + seq_id) * rows).reshape(-1)

    g_blocks = cotangent.reshape(c_size, seqs, t_size, rows, model)
    bit = t_pos % 2

    def parity(block, which):
        pairs = block.reshape(seqs, t_size // 2, 2, rows, model)
        return lax.dynamic_index_in_dim(pairs, which, 2, keepdims=False)

    g_here = pick(g_blocks, c_pos)
    g_same, g_other = [parity(g_here, bit)], [parity(g_here, 1 - bit)]
    for d in range(1, c_size):
        moved = rotate(parity(pick(g_blocks, (c_pos - d) % c_size), bit), "ctx", -d)
        g_same.append(moved)
        g_other.append(swap_tensor(moved, 1))
    g_parts = []
    for offset in rel:
        source = g_same if offset % 2 == 0 else g_other
        index = (t_pos ^ offset) // 2
        for d in range(c_size):
            g_parts.append(lax.dynamic_index_in_dim(source[d], index, 1, keepdims=False))
    grad_all = jnp.concatenate(g_parts, axis=0).reshape(-1, model)
    span_rows = own_rows.shape[0]

    rows_in = own_rows.astype(F32)
    normed_all, inv_all = layer_stats(tokens_all.astype(F32))
    norm_one = (normed_all * gain_one + shift_one).astype(BF16)
    normed_one, inv_one = layer_stats(rows_in)
    qkv = (dot(norm_one, w_heads) + b_heads).astype(BF16)
    q_pos, k_pos, v_pos, out_t, lse, attn = attend(starts, qkv, seqs, pieces)
    merged = scatter_tensor(attn, w_merge_t.T)
    resid = rows_in + merged + b_merge

    normed_two, inv_two = layer_stats(resid)
    norm_two = gather_tensor((normed_two * gain_two + shift_two).astype(BF16))
    grad_act = dot(grad_all, w_down_t)
    pre = dot(norm_two, w_up) + b_up
    tangent = jnp.tanh(GELU_C * (pre + 0.044715 * pre * pre * pre))
    activ = (0.5 * pre * (1.0 + tangent)).astype(BF16)
    slope = 0.5 * (1.0 + tangent) + 0.5 * pre * (1.0 - tangent * tangent) * GELU_C * (
        1.0 + 3.0 * 0.044715 * pre * pre
    )
    grad_pre = grad_act * slope
    grad_up_bias = jnp.sum(grad_pre, axis=0)
    grad_pre_low = grad_pre.astype(BF16)
    grad_norm_two = scatter_tensor(grad_pre_low, w_up.T)

    own_grad = grad_all[:span_rows].astype(F32)
    grad_resid = own_grad + norm_back(grad_norm_two, normed_two, inv_two, gain_two)
    grad_resid_all = gather_tensor(grad_resid.astype(BF16))
    mixed = scatter_tensor(activ, w_down_t.T)
    block_rows = (resid + mixed + b_down).astype(BF16)

    grad_attn = dot(grad_resid_all, w_merge_t).astype(BF16)
    grad_up = dot(norm_two, grad_pre_low, ((0,), (0,)))
    grad_down_t = dot(grad_all, activ, ((0,), (0,)))
    grad_merge_t = dot(grad_resid_all, attn, ((0,), (0,)))
    second_grad = jnp.concatenate([grad_up, grad_down_t, grad_merge_t], axis=1).astype(BF16)
    second_own = lax.psum_scatter(
        second_grad, ("dp", "ctx"), scatter_dimension=0, tiled=True
    ).astype(F32)

    grad_qkv, bias_sum = attend_back(
        starts, grad_attn, q_pos, k_pos, v_pos, out_t, lse, pieces
    )
    grad_norm_one = scatter_tensor(grad_qkv, w_heads.T)
    grad_heads = dot(norm_one, grad_qkv, ((0,), (0,)))
    tokens_rows = grad_resid + norm_back(grad_norm_one, normed_one, inv_one, gain_one)

    qkv_sum = dot(jnp.ones((8, grad_qkv.shape[0]), BF16), grad_qkv)[0]
    wide = w_heads.astype(F32)
    shift_one_part = jnp.sum(wide * qkv_sum, axis=1)
    gain_one_part = (jnp.sum(wide * grad_heads, axis=1) - shift_one * shift_one_part) / gain_one
    bias_pair = lax.dynamic_update_slice(
        jnp.zeros((2, model), F32), jnp.sum(bias_sum, axis=0), (0, t_pos * width)
    )
    vec_grads = jnp.stack(
        [
            gain_one_part,
            shift_one_part,
            bias_pair[0],
            bias_pair[1],
            jnp.sum(grad_resid, axis=0),
            jnp.sum(grad_norm_two * normed_two, axis=0),
            jnp.sum(grad_norm_two, axis=0),
            jnp.sum(own_grad, axis=0),
        ]
    )
    vec_grads = jnp.swapaxes(vec_grads.reshape(8, owners, shard), 0, 1).reshape(owners, -1)
    up_bias_pad = lax.dynamic_update_slice(
        jnp.zeros((hidden_all,), F32), grad_up_bias, (t_pos * hidden,)
    ).reshape(owners, -1)
    small = jnp.concatenate([vec_grads, up_bias_pad], axis=1)
    count = small.shape[1]
    lines = -(-count // (3 * width))
    small = jnp.pad(small, ((0, 0), (0, lines * 3 * width - count))).reshape(owners, lines, -1)
    first_grad = jnp.concatenate(
        [grad_heads.reshape(owners, shard, 3 * width), small], axis=1
    ).astype(BF16)
    first_own = scatter_params(first_grad.reshape((dp_size, c_size) + first_grad.shape[1:]))
    heads_own = first_own[:shard]
    small_own = first_own[shard:].reshape(-1)[:count]
    small_low = small_own.astype(BF16)
    small_own = small_own + sum(
        rotate(small_low, "tensor", d).astype(F32) for d in range(1, t_size)
    )
    vec_own = small_own[: 8 * shard].reshape(8, shard)
    up_bias_own = small_own[8 * shard :]

    def send_back(array):
        parts = array.reshape(c_size, seqs, rows, model)
        held = jnp.stack(
            [parts[0]] + [rotate(parts[d], "ctx", d) for d in range(1, c_size)]
        )
        return jnp.concatenate(
            [pick(held, (c_pos - s) % c_size) for s in range(c_size)], axis=0
        )

    block_out = send_back(block_rows)
    tokens_grad = send_back(tokens_rows.astype(BF16)).astype(F32)
    return (
        block_out,
        tokens_grad,
        vec_own[0],
        vec_own[1],
        jnp.swapaxes(heads_own.reshape(shard, 3, width), 0, 1),
        vec_own[2:4],
        second_own[:, 2 * hidden :].T,
        vec_own[4],
        vec_own[5],
        vec_own[6],
        second_own[:, :hidden],
        up_bias_own,
        second_own[:, hidden : 2 * hidden].T,
        vec_own[7],
    )


def solution(mesh):
    both = P(("dp", "ctx"))
    in_specs = (
        P("dp", ("ctx", "tensor"), None),
        P("dp", "ctx", None),
        P("dp", None),
        both,
        both,
        P(None, ("dp", "ctx"), "tensor"),
        P(None, ("dp", "ctx")),
        P("tensor", ("dp", "ctx")),
        both,
        both,
        both,
        P(("dp", "ctx"), "tensor"),
        both,
        P("tensor", ("dp", "ctx")),
        both,
    )
    out_specs = (
        P("dp", ("ctx", "tensor"), None),
        P("dp", ("ctx", "tensor"), None),
        both,
        both,
        P(None, ("dp", "ctx"), "tensor"),
        P(None, ("dp", "ctx")),
        P("tensor", ("dp", "ctx")),
        both,
        both,
        both,
        P(("dp", "ctx"), "tensor"),
        both,
        P("tensor", ("dp", "ctx")),
        both,
    )
    return jax.shard_map(local, mesh=mesh, in_specs=in_specs, out_specs=out_specs, check_vma=False)
```

```python
import functools

import jax
import jax.numpy as jnp
from jax import lax
from jax.experimental import pallas as pl
from jax.experimental.pallas import tpu as pltpu
from jax.sharding import PartitionSpec as P

HEAD_DIM = 64
EPS = 1e-05
GELU_C = 0.7978845608028654
NEG = -1e30
TILE = 256
F32 = jnp.float32
BF16 = jnp.bfloat16


def layer_stats(rows):
    centred = rows - jnp.mean(rows, axis=-1, keepdims=True)
    inv_std = lax.rsqrt(jnp.mean(centred * centred, axis=-1, keepdims=True) + EPS)
    return (centred * inv_std, inv_std)


def norm_back(grad_out, normed, inv_std, gain):
    scaled = grad_out * gain
    return inv_std * (
        scaled
        - jnp.mean(scaled, axis=-1, keepdims=True)
        - normed * jnp.mean(scaled * normed, axis=-1, keepdims=True)
    )


def dot(left, right, dims=((1,), (0,))):
    return lax.dot_general(left, right, (dims, ((), ())), preferred_element_type=F32)


def causal_tile(size):
    key_row = lax.broadcasted_iota(jnp.int32, (size, size), 0)
    query_col = lax.broadcasted_iota(jnp.int32, (size, size), 1)
    return key_row <= query_col


def attend_kernel(dims, scalars, *refs):
    pieces, heads, shard, model, n_tokens, n_packed = dims
    token_parts, refs = refs[:n_tokens], refs[n_tokens:]
    packed_parts, refs = refs[:n_packed], refs[n_packed:]
    norm_one, vectors, heads_t, merge_t, q_pos, k_pos, v_pos, out_t, lse, attn = refs[:10]
    outs = refs[10:14]
    q_t, v_t, k_h, o_nat, tokens, packed, w_wide, w_low, merge, out = refs[14:]
    seq = pl.program_id(0)
    length, width = q_pos.shape
    rows = length // pieces
    blocks = length // TILE
    owners = packed.shape[0]
    first_slot = pl.num_programs(0) * pieces
    t_pos = scalars[first_slot + owners]
    place = 0
    for part in token_parts:
        tokens[place : place + part.shape[0], :] = part[...]
        place += part.shape[0]
    place = 0
    for part in packed_parts:
        packed[place : place + part.shape[0]] = part[...]
        place += part.shape[0]

    def tail_of(owner):
        return packed[scalars[first_slot + owner]].astype(F32)[shard:, :]

    def entry(tail, index):
        return tail[index : index + 1, :shard]

    tails = []
    for i in range(owners):
        block = packed[scalars[first_slot + i]].astype(F32)
        w_wide[i * shard : (i + 1) * shard, :] = block[:shard, :]
        tails.append(block[shard:, :])
    w_low[...] = w_wide[:, : 3 * width].astype(BF16)
    heads_t[...] = w_wide[:, : 3 * width].T.astype(BF16)
    merge_low = w_wide[:, 3 * width :]
    merge_t[...] = merge_low.astype(BF16)
    merge[...] = merge_low.T.astype(BF16)
    lines = [jnp.concatenate([entry(t, v) for t in tails], axis=1) for v in range(8)]
    group = width // shard
    mine = [tail_of(t_pos * group + k) for k in range(group)]
    bias_q = jnp.concatenate([entry(t, 2) for t in mine], axis=1)
    bias_v = jnp.concatenate([entry(t, 3) for t in mine], axis=1)
    long = model // width * shard
    bias_up = jnp.concatenate([t[8:9, :long] for t in mine], axis=1)
    lines.append(bias_up)
    lines.append(jnp.zeros((16 - len(lines), model), F32))
    vectors[...] = jnp.concatenate(lines, axis=0)
    bias = jnp.concatenate([bias_q, jnp.zeros((1, width), F32), bias_v], axis=1)
    gain, shift = lines[0], lines[1]
    for p in range(pieces):
        first = pl.multiple_of(scalars[seq * pieces + p], rows)
        normed, unused = layer_stats(tokens[pl.ds(first, rows), :].astype(F32))
        normed = (normed * gain + shift).astype(BF16)
        norm_one[pl.ds(first, rows), :] = normed
        part = (dot(normed, w_low[...]) + bias).astype(BF16)
        here = slice(p * rows, (p + 1) * rows)
        q_pos[here, :] = part[:, :width] * jnp.asarray(HEAD_DIM ** (-0.5), BF16)
        k_pos[here, :] = part[:, width : 2 * width]
        v_pos[here, :] = part[:, 2 * width :]
    for b in range(blocks):
        here = slice(b * TILE, (b + 1) * TILE)
        q_t[:, here] = q_pos[here, :].T
        v_t[:, here] = v_pos[here, :].T
        key = k_pos[here, :]
        for h in range(heads):
            k_h[h, here, :] = key[:, h * HEAD_DIM : (h + 1) * HEAD_DIM]
    allowed = causal_tile(TILE)

    def one_head(h, unused):
        hs = pl.ds(pl.multiple_of(h * HEAD_DIM, HEAD_DIM), HEAD_DIM)
        for i in range(blocks):
            here = slice(i * TILE, (i + 1) * TILE)
            query = q_t[hs, here]
            diag = jnp.where(allowed, dot(k_h[h, here, :], query), NEG)
            top = jnp.max(diag, axis=0, keepdims=True)
            if i > 0:
                past = dot(k_h[h, : i * TILE, :], query)
                top = jnp.maximum(top, jnp.max(past, axis=0, keepdims=True))
            diag = jnp.exp(diag - top)
            total = jnp.sum(diag, axis=0, keepdims=True)
            mixed = dot(v_t[hs, here], diag.astype(BF16))
            if i > 0:
                past = jnp.exp(past - top)
                total += jnp.sum(past, axis=0, keepdims=True)
                mixed += dot(v_t[hs, : i * TILE], past.astype(BF16))
            out_t[hs, here] = mixed / total
            lse[h, :, here] = top + jnp.log(total)
        return unused

    lax.fori_loop(0, heads, one_head, 0)
    for b in range(blocks):
        here = slice(b * TILE, (b + 1) * TILE)
        o_nat[here, :] = out_t[:, here].T.astype(BF16)
    for p in range(pieces):
        first = pl.multiple_of(scalars[seq * pieces + p], rows)
        part = o_nat[p * rows : (p + 1) * rows, :]
        attn[pl.ds(first, rows), :] = part
        out[pl.ds(first, rows), :] = dot(part, merge[...]).astype(BF16)
    size = out.shape[0] // 4
    for j in range(4):
        outs[j][...] = out[j * size : (j + 1) * size, :]


def attend(scalars, token_parts, packed_parts, shard, width, seqs, pieces):
    total = sum(p.shape[0] for p in token_parts)
    model = token_parts[0].shape[1]
    owners = sum(p.shape[0] for p in packed_parts)
    heads = width // HEAD_DIM
    length = total // seqs
    nat = jax.ShapeDtypeStruct((seqs, length, width), BF16)
    nat_spec = pl.BlockSpec((None, length, width), lambda s, t: (s, 0, 0))
    pairs = heads * length * (length + TILE) // 2 * seqs
    whole = lambda *shape: pl.BlockSpec(shape, lambda s, t: (0,) * len(shape))
    return pl.pallas_call(
        functools.partial(
            attend_kernel, (pieces, heads, shard, model, len(token_parts), len(packed_parts))
        ),
        grid_spec=pltpu.PrefetchScalarGridSpec(
            num_scalar_prefetch=1,
            grid=(seqs,),
            in_specs=[whole(*p.shape) for p in token_parts + packed_parts],
            out_specs=[
                whole(total, model),
                whole(16, model),
                whole(3 * width, model),
                whole(model, width),
                nat_spec,
                nat_spec,
                nat_spec,
                pl.BlockSpec((None, width, length), lambda s, t: (s, 0, 0)),
                pl.BlockSpec((None, heads, 1, length), lambda s, t: (s, 0, 0, 0)),
                whole(total, width),
            ]
            + [whole(total // 4, model)] * 4,
            scratch_shapes=[
                pltpu.VMEM((width, length), BF16),
                pltpu.VMEM((width, length), BF16),
                pltpu.VMEM((heads, length, HEAD_DIM), BF16),
                pltpu.VMEM((length, width), BF16),
                pltpu.VMEM((total, model), BF16),
                pltpu.VMEM((owners,) + packed_parts[0].shape[1:], BF16),
                pltpu.VMEM((model, 4 * width), F32),
                pltpu.VMEM((model, 3 * width), BF16),
                pltpu.VMEM((width, model), BF16),
                pltpu.VMEM((total, model), BF16),
            ],
        ),
        out_shape=[
            jax.ShapeDtypeStruct((total, model), BF16),
            jax.ShapeDtypeStruct((16, model), F32),
            jax.ShapeDtypeStruct((3 * width, model), BF16),
            jax.ShapeDtypeStruct((model, width), BF16),
            nat,
            nat,
            nat,
            jax.ShapeDtypeStruct((seqs, width, length), F32),
            jax.ShapeDtypeStruct((seqs, heads, 1, length), F32),
            jax.ShapeDtypeStruct((total, width), BF16),
        ]
        + [jax.ShapeDtypeStruct((total // 4, model), BF16)] * 4,
        compiler_params=pltpu.CompilerParams(vmem_limit_bytes=58 * 2**20),
        cost_estimate=pl.CostEstimate(
            flops=32 * HEAD_DIM * pairs, bytes_accessed=24 * total * model, transcendentals=pairs
        ),
        name="attend",
    )(scalars, *token_parts, *packed_parts)


def attend_back_kernel(dims, starts, *refs):
    pieces, heads, shard, ctx, t_index = dims
    row_parts, refs = refs[:4], refs[4:]
    merge_t, heads_t, norm_one, attn, q_pos, k_pos, v_pos, out_t, lse = refs[:9]
    vectors, resid_sums, up_n, up_2, up_3 = refs[9:14]
    backs, weights = refs[14:18], refs[18]
    grad_rows, do_nat, q_t, k_t, do_t, q_h, k_h, v_h, do_h, row_dot, dq_t, dk_h, dv_h, g_nat = (
        refs[19:33]
    )
    g_t, back, w_full = refs[33:]
    t_pos = starts[t_index]
    seq = pl.program_id(0)
    length, width = q_pos.shape
    model = norm_one.shape[1]
    rows = length // pieces
    blocks = length // TILE
    place = 0
    for part in row_parts:
        grad_rows[place : place + part.shape[0], :] = part[...]
        place += part.shape[0]
    for p in range(pieces):
        first = pl.multiple_of(starts[seq * pieces + p], rows)
        part = dot(grad_rows[pl.ds(first, rows), :], merge_t[...])
        do_nat[p * rows : (p + 1) * rows, :] = part.astype(BF16)
    for b in range(blocks):
        here = slice(b * TILE, (b + 1) * TILE)
        query, key, value, grad = q_pos[here, :], k_pos[here, :], v_pos[here, :], do_nat[here, :]
        q_t[:, here] = query.T
        k_t[:, here] = key.T
        grad_t = grad.T
        do_t[:, here] = grad_t
        product = grad_t.astype(F32) * out_t[:, here]
        for h in range(heads):
            cols = slice(h * HEAD_DIM, (h + 1) * HEAD_DIM)
            q_h[h, here, :] = query[:, cols]
            k_h[h, here, :] = key[:, cols]
            v_h[h, here, :] = value[:, cols]
            do_h[h, here, :] = grad[:, cols]
            row_dot[h, :, here] = jnp.sum(product[cols, :], axis=0, keepdims=True)
    allowed = causal_tile(TILE)

    def one_head(h, unused):
        hs = pl.ds(pl.multiple_of(h * HEAD_DIM, HEAD_DIM), HEAD_DIM)
        for j in range(blocks):
            here = slice(j * TILE, (j + 1) * TILE)
            key, value = k_h[h, here, :], v_h[h, here, :]
            key_t = k_t[hs, here]
            scores = jnp.where(allowed, dot(key, q_t[hs, here]), NEG)
            probs = jnp.exp(scores - lse[h, :, here])
            slope = probs * (dot(value, do_t[hs, here]) - row_dot[h, :, here])
            slope_low = slope.astype(BF16)
            grad_v = dot(probs.astype(BF16), do_h[h, here, :])
            grad_k = dot(slope_low, q_h[h, here, :])
            add = dot(key_t, slope_low)
            dq_t[hs, here] = add if j == 0 else dq_t[hs, here] + add
            if j < blocks - 1:
                later = slice((j + 1) * TILE, length)
                probs = jnp.exp(dot(key, q_t[hs, later]) - lse[h, :, later])
                slope = probs * (dot(value, do_t[hs, later]) - row_dot[h, :, later])
                slope_low = slope.astype(BF16)
                grad_v += dot(probs.astype(BF16), do_h[h, later, :])
                grad_k += dot(slope_low, q_h[h, later, :])
                add = dot(key_t, slope_low)
                dq_t[hs, later] = add if j == 0 else dq_t[hs, later] + add
            dk_h[h, here, :] = grad_k
            dv_h[h, here, :] = grad_v
        return unused

    lax.fori_loop(0, heads, one_head, 0)
    wide = jnp.zeros((1, 3 * width), F32)
    for b in range(blocks):
        here = slice(b * TILE, (b + 1) * TILE)
        grad_q = dq_t[:, here].T * (HEAD_DIM ** (-0.5))
        grad_k = jnp.concatenate([dk_h[h, here, :] for h in range(heads)], axis=1)
        grad_v = jnp.concatenate([dv_h[h, here, :] for h in range(heads)], axis=1)
        grads = jnp.concatenate([grad_q, grad_k, grad_v], axis=1)
        wide += jnp.sum(grads, axis=0, keepdims=True)
        g_nat[here, :] = grads.astype(BF16)
    w_t = jnp.zeros((3 * width, model), F32)
    m_t = jnp.zeros((width, model), F32)
    column = jnp.zeros((3 * width, 1), F32)
    for p in range(pieces):
        first = pl.multiple_of(starts[seq * pieces + p], rows)
        part = g_nat[p * rows : (p + 1) * rows, :]
        back[pl.ds(first, rows), :] = dot(part, heads_t[...]).astype(BF16)
    for p in range(pieces):
        first = pl.multiple_of(starts[seq * pieces + p], rows)
        g_t[:, :] = g_nat[p * rows : (p + 1) * rows, :].astype(F32).T
        turned = g_t[...]
        column += jnp.sum(turned, axis=1, keepdims=True)
        w_t += dot(turned.astype(BF16), norm_one[pl.ds(first, rows), :])
        mine = attn[pl.ds(first, rows), :].astype(F32).T.astype(BF16)
        m_t += dot(mine, grad_rows[pl.ds(first, rows), :])
    w_full[:, : 3 * width] = w_t.T
    w_full[:, 3 * width :] = m_t.T
    size = back.shape[0] // 4
    for j in range(4):
        backs[j][...] = back[j * size : (j + 1) * size, :]
    factor = heads_t[...].astype(F32)
    group = lax.broadcasted_iota(jnp.int32, (1, model), 1) // width
    spread = lambda part: jnp.where(
        group == t_pos, jnp.concatenate([part] * (model // width), axis=1), 0.0
    )
    shift_sum = jnp.sum(factor * column, axis=0, keepdims=True)
    gain_sum = jnp.sum(factor * w_t, axis=0, keepdims=True) - vectors[1:2, :] * shift_sum
    up_sum = up_n[...] + up_2[...] + up_3[...]
    lines = jnp.concatenate(
        [
            gain_sum / vectors[0:1, :],
            shift_sum,
            spread(wide[:, :width]),
            spread(wide[:, 2 * width :]),
            resid_sums[0:4, :],
        ],
        axis=0,
    )
    owners = model // shard
    long = model // width * shard
    for i in range(owners):
        k, lane = i * long // model, i * long % model
        here = slice(i * shard, (i + 1) * shard)
        block = [
            w_full[here, :],
            jnp.concatenate([lines[:, here], jnp.zeros((8, model - shard), F32)], axis=1),
            jnp.concatenate(
                [
                    jnp.where(t_pos == k, up_sum[:, lane : lane + long], 0.0),
                    jnp.zeros((1, model - long), F32),
                ],
                axis=1,
            ),
            jnp.zeros((7, model), F32),
        ]
        weights[i % ctx, i // ctx] = jnp.concatenate(block, axis=0).astype(BF16)


def attend_back(starts, row_parts, merge_t, heads_t, norm_one, attn, kept, lines, shard, ctx, pieces):
    q_pos, k_pos, v_pos, out_t, lse = kept
    total, model = norm_one.shape
    width = merge_t.shape[1]
    seqs, length, unused = q_pos.shape
    heads = width // HEAD_DIM
    nat_spec = pl.BlockSpec((None, length, width), lambda s, t: (s, 0, 0))
    whole = lambda *shape: pl.BlockSpec(shape, lambda s, t: (0,) * len(shape))
    pairs = heads * length * (length + TILE) // 2 * seqs
    per_head = pltpu.VMEM((heads, length, HEAD_DIM), BF16)
    by_owner = (ctx, model // shard // ctx, shard + 16, 4 * width)
    across = pltpu.VMEM((width, length), BF16)
    return pl.pallas_call(
        functools.partial(
            attend_back_kernel, (pieces, heads, shard, ctx, starts.shape[0] - 1)
        ),
        grid_spec=pltpu.PrefetchScalarGridSpec(
            num_scalar_prefetch=1,
            grid=(seqs,),
            in_specs=[whole(*p.shape) for p in row_parts]
            + [
                whole(model, width),
                whole(3 * width, model),
                whole(total, model),
                whole(total, width),
                nat_spec,
                nat_spec,
                nat_spec,
                pl.BlockSpec((None, width, length), lambda s, t: (s, 0, 0)),
                pl.BlockSpec((None, heads, 1, length), lambda s, t: (s, 0, 0, 0)),
            ]
            + [whole(*v.shape) for v in lines],
            out_specs=[whole(total // 4, model)] * 4
            + [
                pl.BlockSpec((None,) + by_owner, lambda s, t: (s, 0, 0, 0, 0)),
            ],
            scratch_shapes=[
                pltpu.VMEM((total, model), BF16),
                pltpu.VMEM((length, width), BF16),
                across,
                across,
                across,
                per_head,
                per_head,
                per_head,
                per_head,
                pltpu.VMEM((heads, 1, length), F32),
                pltpu.VMEM((width, length), F32),
                pltpu.VMEM((heads, length, HEAD_DIM), F32),
                pltpu.VMEM((heads, length, HEAD_DIM), F32),
                pltpu.VMEM((length, 3 * width), BF16),
                pltpu.VMEM((3 * width, length // pieces), F32),
                pltpu.VMEM((total, model), BF16),
                pltpu.VMEM((model, 4 * width), F32),
            ],
        ),
        out_shape=[jax.ShapeDtypeStruct((total // 4, model), BF16)] * 4
        + [
            jax.ShapeDtypeStruct((seqs,) + by_owner, BF16),
        ],
        compiler_params=pltpu.CompilerParams(vmem_limit_bytes=60 * 2**20),
        cost_estimate=pl.CostEstimate(
            flops=60 * HEAD_DIM * pairs, bytes_accessed=24 * total * model, transcendentals=pairs
        ),
        name="attend_back",
    )(starts, *row_parts, merge_t, heads_t, norm_one, attn, q_pos, k_pos, v_pos, out_t, lse, *lines)


def feed_kernel(
    seqs,
    ctx,
    turned,
    table,
    norm,
    g_own,
    g_far,
    up,
    down_t,
    bias,
    *refs,
):
    step = pl.program_id(0)
    if turned:
        up_t, down, act, pre_low, back, mix, g_out, sums = refs
    else:
        act, pre_low, back, mix, g_out, sums, up_t, down = refs

        @pl.when(step == 0)
        def turn_weights():
            up_t[...] = up[...].T
            down[...] = down_t[...].T

    distance = lax.rem(lax.div(step, seqs), ctx)
    grad = jnp.where(distance == 0, g_own[...], g_far[...])
    g_out[...] = grad
    pre = dot(norm[...], up[...]) + bias[...]
    grad_act = dot(grad, down_t[...])
    square = pre * pre
    tangent = jnp.tanh(GELU_C * (pre + 0.044715 * square * pre))
    half = 0.5 * (1.0 + tangent)
    low_act = (pre * half).astype(BF16)
    act[...] = low_act
    mix[...] = dot(low_act, down[...]).astype(BF16)
    slope = half + 0.5 * pre * (1.0 - tangent * tangent) * (
        GELU_C + (GELU_C * 3.0 * 0.044715) * square
    )
    grad_pre = grad_act * slope
    total = jnp.sum(grad_pre, axis=0, keepdims=True)
    sums[...] = jnp.where(step == 0, total, sums[...] + total)
    low = grad_pre.astype(BF16)
    pre_low[...] = low
    back[...] = dot(low, up_t[...]).astype(BF16)


def feed(table, norm, g_own, g_far, second, bias, turned, seqs, ctx):
    total, model = norm.shape
    rows = g_own.shape[1]
    hidden = second.shape[1] // 2
    steps = total // rows
    by_rows = lambda size: pl.BlockSpec((rows, size), lambda i, t: (i, 0))
    return pl.pallas_call(
        functools.partial(feed_kernel, seqs, ctx, len(turned) > 0),
        grid_spec=pltpu.PrefetchScalarGridSpec(
            num_scalar_prefetch=1,
            grid=(steps,),
            in_specs=[
                by_rows(model),
                pl.BlockSpec((None, rows, model), lambda i, t: (t[i], 0, 0)),
                pl.BlockSpec((None, rows, model), lambda i, t: (t[steps + i], 0, 0)),
                pl.BlockSpec((model, hidden), lambda i, t: (0, 0)),
                pl.BlockSpec((model, hidden), lambda i, t: (0, 1)),
                pl.BlockSpec((1, hidden), lambda i, t: (0, 0)),
            ]
            + [pl.BlockSpec((hidden, model), lambda i, t: (0, 0))] * len(turned),
            out_specs=[
                by_rows(hidden),
                by_rows(hidden),
                by_rows(model),
                by_rows(model),
                by_rows(model),
                pl.BlockSpec((1, hidden), lambda i, t: (0, 0)),
            ]
            + [pl.BlockSpec((hidden, model), lambda i, t: (0, 0))] * (2 - len(turned)),
        ),
        out_shape=[
            jax.ShapeDtypeStruct((total, hidden), BF16),
            jax.ShapeDtypeStruct((total, hidden), BF16),
            jax.ShapeDtypeStruct((total, model), BF16),
            jax.ShapeDtypeStruct((total, model), BF16),
            jax.ShapeDtypeStruct((total, model), BF16),
            jax.ShapeDtypeStruct((1, hidden), F32),
        ]
        + [jax.ShapeDtypeStruct((hidden, model), BF16)] * (2 - len(turned)),
        compiler_params=pltpu.CompilerParams(vmem_limit_bytes=60 * 2**20),
        cost_estimate=pl.CostEstimate(
            flops=8 * total * model * hidden,
            bytes_accessed=14 * total * model,
            transcendentals=total * hidden,
        ),
        name="feed",
    )(table, norm, g_own, g_far, second, second, bias, *turned)


def resid_kernel(own, beside, across, resid, grad, vectors, out, low, sums):
    step = pl.program_id(0)
    normed, inv_std = layer_stats(resid[...])
    back = own[...].astype(F32) + beside[...].astype(F32) + across[...].astype(F32)
    given = grad[...].astype(F32)
    total = given + norm_back(back, normed, inv_std, vectors[5:6, :])
    out[...] = total
    low[...] = total.astype(BF16)
    add = lambda rows: jnp.sum(rows, axis=0, keepdims=True)
    lines = jnp.concatenate(
        [add(total), add(back * normed), add(back), add(given), jnp.zeros((4, total.shape[1]), F32)],
        axis=0,
    )
    sums[...] = jnp.where(step == 0, lines, sums[...] + lines)


def first_kernel(own, beside, across, rows, grad, vectors, out, low):
    normed, inv_std = layer_stats(rows[...].astype(F32))
    back = own[...].astype(F32) + beside[...].astype(F32) + across[...].astype(F32)
    total = grad[...] + norm_back(back, normed, inv_std, vectors[0:1, :])
    out[...] = total
    low[...] = total.astype(BF16)


def row_wise(kernel, parts, vectors, with_sums):
    total, model = parts[3].shape
    steps = 4
    by_rows = pl.BlockSpec((total // steps, model), lambda i: (i, 0))
    fixed = lambda rows: pl.BlockSpec((rows, model), lambda i: (0, 0))
    return pl.pallas_call(
        kernel,
        grid=(steps,),
        in_specs=[by_rows] * len(parts) + [fixed(16)],
        out_specs=[by_rows, by_rows] + [fixed(8)] * with_sums,
        out_shape=[
            jax.ShapeDtypeStruct((total, model), F32),
            jax.ShapeDtypeStruct((total, model), BF16),
        ]
        + [jax.ShapeDtypeStruct((8, model), F32)] * with_sums,
        cost_estimate=pl.CostEstimate(
            flops=20 * total * model, bytes_accessed=18 * total * model, transcendentals=total
        ),
        name="row_wise",
    )(*parts, vectors)


def heads_kernel(width, a, b, c, d, heads, merge, small):
    shard = merge.shape[1]
    total = sum(part[...].astype(F32) for part in (a, b, c, d))
    for m in range(3):
        heads[m] = total[:shard, m * width : (m + 1) * width]
    merge[...] = total[:shard, 3 * width :].T
    small[...] = total[shard:, :]


def finish_heads(parts, width):
    shard = parts[0].shape[0] - 16
    if len(parts) != 4:
        low = [sum(p.astype(F32) for p in parts)] + [jnp.zeros(parts[0].shape, F32)] * 3
        parts = low
    return pl.pallas_call(
        functools.partial(heads_kernel, width),
        out_shape=[
            jax.ShapeDtypeStruct((3, shard, width), F32),
            jax.ShapeDtypeStruct((width, shard), F32),
            jax.ShapeDtypeStruct((16, 4 * width), F32),
        ],
        name="finish_heads",
    )(*parts)


def swap_tensor(block, bit):
    size = lax.axis_size("tensor")
    return lax.ppermute(block, "tensor", [(i, i ^ bit) for i in range(size)])


def rotate(block, axis, distance):
    size = lax.axis_size(axis)
    return lax.ppermute(block, axis, [(i, (i + distance) % size) for i in range(size)])


def scatter_tensor(parts):
    far = swap_tensor(parts[3], 1)
    near = (parts[2].astype(F32) + far.astype(F32)).astype(BF16)
    across = swap_tensor(near, 2)
    beside = swap_tensor(parts[1], 1)
    return (parts[0], beside, across)


def quarters(rows):
    size = rows.shape[0] // 4
    return [rows[j * size : (j + 1) * size] for j in range(4)]


def add_all(parts):
    return sum(p.astype(F32) for p in parts)


def pick(array, index):
    return lax.dynamic_index_in_dim(array, index, 0, keepdims=False)


def scatter_ctx(blocks):
    ctx, ctx_pos = lax.axis_size("ctx"), lax.axis_index("ctx")
    take = lambda c: lax.dynamic_index_in_dim(blocks, c, 1, keepdims=False)
    total = take(ctx_pos).astype(F32)
    for d in range(1, ctx):
        total += rotate(take((ctx_pos + d) % ctx), "ctx", d).astype(F32)
    return total.astype(BF16)


def scatter_dp(blocks):
    dp, dp_pos = lax.axis_size("dp"), lax.axis_index("dp")
    return [pick(blocks, dp_pos)] + [
        rotate(pick(blocks, (dp_pos + d) % dp), "dp", d) for d in range(1, dp)
    ]


def local(
    tokens,
    cotangent,
    stretch_order,
    attn_gain,
    attn_shift,
    heads_weight,
    heads_bias,
    merge_weight,
    merge_bias,
    feed_gain,
    feed_shift,
    up_weight,
    up_bias,
    down_weight,
    down_bias,
):
    t_size, t_pos = lax.axis_size("tensor"), lax.axis_index("tensor")
    c_size, c_pos = lax.axis_size("ctx"), lax.axis_index("ctx")
    dp_size, dp_pos = lax.axis_size("dp"), lax.axis_index("dp")
    owners = dp_size * c_size
    seqs_in, rows, model = tokens.shape
    seqs = seqs_in // c_size
    shard = heads_weight.shape[1]
    width = heads_weight.shape[2]
    hidden = up_weight.shape[1]
    hidden_all = hidden * t_size
    pieces = c_size * t_size
    span_rows = c_size * seqs * rows

    by_owner = tokens.reshape(c_size, seqs, rows, model)
    near = pick(by_owner, c_pos).reshape(-1, model)
    far = [rotate(pick(by_owner, (c_pos - d) % c_size), "ctx", -d) for d in range(1, c_size)]
    far = jnp.concatenate(far, axis=0).reshape(-1, model)
    near_x = swap_tensor(near, 2)
    far_x = swap_tensor(far, 2)
    own_rows = jnp.concatenate([near, far], axis=0)

    line = lax.broadcasted_iota(jnp.int32, (16, model), 0)
    small = jnp.zeros((16, model), BF16)
    for index, vector in enumerate(
        [
            attn_gain,
            attn_shift,
            heads_bias[0],
            heads_bias[1],
            merge_bias,
            feed_gain,
            feed_shift,
            down_bias,
            up_bias,
        ]
    ):
        wide = jnp.pad(vector, (0, model - vector.shape[0]))
        small = jnp.where(line == index, wide[None, :], small)
    first_pack = jnp.concatenate(
        [
            jnp.concatenate(
                [heads_weight[0], heads_weight[1], heads_weight[2], merge_weight.T], axis=1
            ),
            small,
        ],
        axis=0,
    )
    by_dp = [first_pack] + [rotate(first_pack, "dp", -d) for d in range(1, dp_size)]
    packed_parts = by_dp + [rotate(p, "ctx", -d) for d in range(1, c_size) for p in by_dp]
    second_pack = jnp.concatenate([up_weight, down_weight.T], axis=1)
    second_pack, by_dp[-1] = lax.optimization_barrier((second_pack, by_dp[-1]))
    packed_parts = [p[None] for p in packed_parts]
    second_all = lax.all_gather(second_pack, ("dp", "ctx"), axis=0, tiled=True)

    near_1, far_1 = swap_tensor(near, 1), swap_tensor(far, 1)
    near_3, far_3 = swap_tensor(near_x, 1), swap_tensor(far_x, 1)
    token_parts = [near, far, near_1, far_1, near_x, far_x, near_3, far_3]

    per_stretch = t_size // 2
    order = lax.dynamic_slice_in_dim(stretch_order, c_pos * seqs, seqs, 0)
    stretches = order.shape[1]
    span = jnp.arange(stretches, dtype=jnp.int32)
    inverse = jnp.sum(
        jnp.where(order[:, :, None] == span[None, None, :], span[None, :, None], 0), axis=1
    )
    stored = inverse[:, :, None]
    part = jnp.arange(per_stretch, dtype=jnp.int32)[None, None, :]
    slot = ((stored % 2) * per_stretch + part) ^ t_pos
    away = (stored // 2 - c_pos) % c_size
    seq_id = jnp.arange(seqs, dtype=jnp.int32)[:, None, None]
    starts = (((slot * c_size + away) * seqs + seq_id) * rows).reshape(-1)
    owner = jnp.arange(owners, dtype=jnp.int32)
    slots = ((owner % c_size - c_pos) % c_size) * dp_size + (owner // c_size - dp_pos) % dp_size
    scalars = jnp.concatenate([starts, slots, t_pos[None].astype(jnp.int32)])

    g_blocks = cotangent.reshape(c_size, seqs, 2, t_size // 2, rows, model)
    bit = t_pos % 2
    g_moved = [
        rotate(
            lax.dynamic_index_in_dim(pick(g_blocks, (c_pos - d) % c_size), bit, 1, keepdims=False),
            "ctx",
            -d,
        )
        for d in range(1, c_size)
    ]
    g_moved = jnp.stack(g_moved)

    norm_one, vec, heads_t, merge_t, q_pos, k_pos, v_pos, out_t, lse, attn, *shares = attend(
        scalars, token_parts, packed_parts, shard, width, seqs, pieces
    )
    shares[3], g_moved = lax.optimization_barrier((shares[3], g_moved))
    merged = add_all(scatter_tensor(shares))
    b_merge, gain_two, shift_two, b_down = vec[4], vec[5], vec[6], vec[7]
    rows_in = own_rows.astype(F32)
    resid = rows_in + merged + b_merge

    normed_two, inv_two = layer_stats(resid)
    norm_0 = (normed_two * gain_two + shift_two).astype(BF16)
    norm_2 = swap_tensor(norm_0, 2)
    norm_near = jnp.concatenate([norm_0, swap_tensor(norm_0, 1)], axis=0)
    g_own = cotangent.reshape(-1, rows, model)
    g_far = jnp.stack([g_moved, swap_tensor(g_moved, 1)], axis=2).reshape(-1, rows, model)
    b_up = vec[8:9, :hidden]

    def feed_part(offsets, norm, turned=()):
        own_table, far_table = [], []
        for j in offsets:
            piece = t_pos ^ j
            for d in range(c_size):
                for q in range(seqs):
                    own_table.append((c_pos * seqs + q) * t_size + piece if d == 0 else 0 * piece)
                    place = (piece // 2) ^ bit
                    far_row = (((d - 1) * seqs + q) * 2 + place) * (t_size // 2) + piece % 2
                    far_table.append(far_row if d > 0 else 0 * piece)
        table = jnp.stack(own_table + far_table).astype(jnp.int32)
        return feed(table, norm, g_own, g_far, second_all, b_up, turned, seqs, c_size)

    act_n, pre_n, back_n, mix_n, g_n, up_sum_n, *turned = feed_part((0, 1), norm_near)
    norm_2, up_sum_n = lax.optimization_barrier((norm_2, up_sum_n))
    norm_3 = swap_tensor(norm_2, 1)
    act_3, pre_3, back_3, mix_3, g_3, up_sum_3 = feed_part((3,), norm_3, turned)
    act_2, pre_2, back_2, mix_2, g_2, up_sum_2 = feed_part((2,), norm_2, turned)
    unused, beside, across = scatter_tensor([back_n, back_n[span_rows:], back_2, back_3])

    together = lambda parts: jnp.concatenate(parts, axis=0)
    grad_down_t = dot(together([g_n, g_2, g_3]), together([act_n, act_2, act_3]), ((0,), (0,)))
    grad_up = dot(together([norm_near, norm_2, norm_3]), together([pre_n, pre_2, pre_3]), ((0,), (0,)))
    feed_grad = jnp.concatenate([grad_up, grad_down_t], axis=1).astype(BF16)
    across, feed_grad = lax.optimization_barrier((across, feed_grad))
    feed_half = scatter_ctx(feed_grad.reshape(dp_size, c_size, shard, 2 * hidden))
    grad_resid, resid_0, resid_sums = row_wise(
        resid_kernel, [back_n, beside, across, resid, g_n], vec, True
    )
    resid_2 = swap_tensor(resid_0, 2)
    resid_1 = swap_tensor(resid_0, 1)
    mix_beside = swap_tensor(mix_n[span_rows:], 1)
    mix_near = (mix_2.astype(F32) + swap_tensor(mix_3, 1).astype(F32)).astype(BF16)
    resid_2, mix_near, feed_half = lax.optimization_barrier((resid_2, mix_near, feed_half))
    mix_across = swap_tensor(mix_near, 2)
    feed_parts = scatter_dp(feed_half)

    *backs, weights = attend_back(
        scalars,
        [resid_0, resid_1, resid_2, swap_tensor(resid_2, 1)],
        merge_t,
        heads_t,
        norm_one,
        attn,
        (q_pos, k_pos, v_pos, out_t, lse),
        [vec, resid_sums, up_sum_n, up_sum_2, up_sum_3],
        shard,
        c_size,
        pieces,
    )
    weights, feed_parts, mix_across = lax.optimization_barrier((weights, feed_parts, mix_across))
    unused, beside, across = scatter_tensor(backs)
    tokens_rows, tokens_low = row_wise(
        first_kernel, [backs[0], beside, across, own_rows, grad_resid], vec, False
    )
    if seqs == 1:
        weights = weights[0]
    else:
        weights = jnp.sum(weights.astype(F32), axis=0).astype(BF16)
    heads_half = pick(weights, c_pos).astype(F32)
    for d in range(1, c_size):
        heads_half += rotate(pick(weights, (c_pos + d) % c_size), "ctx", d).astype(F32)
    heads_half = heads_half.astype(BF16)
    heads_own, merge_own, sums = finish_heads(scatter_dp(heads_half), width)
    feed_own = add_all(feed_parts)
    up_own, down_own = feed_own[:, :hidden], feed_own[:, hidden:]
    mixed = add_all([mix_n[:span_rows], mix_beside, mix_across])
    block_rows = (resid + mixed + b_down).astype(BF16)
    block_rows, heads_half = lax.optimization_barrier((block_rows, heads_half))

    sums = add_all([sums] + [rotate(sums, "tensor", d) for d in range(1, t_size)])
    vec_own = sums[:8, :shard]
    up_bias_own = sums[8, : hidden_all // owners]

    def send_back(low, own):
        parts = low.reshape(c_size, seqs, rows, model)
        held = jnp.stack(
            [own.reshape(c_size, seqs, rows, model)[0]]
            + [rotate(parts[d], "ctx", d).astype(own.dtype) for d in range(1, c_size)]
        )
        return jnp.concatenate(
            [pick(held, (c_pos - s) % c_size) for s in range(c_size)], axis=0
        )

    block_out = send_back(block_rows, block_rows)
    tokens_grad = send_back(tokens_low, tokens_rows)
    return (
        block_out,
        tokens_grad,
        vec_own[0],
        vec_own[1],
        heads_own,
        vec_own[2:4],
        merge_own,
        vec_own[4],
        vec_own[5],
        vec_own[6],
        up_own,
        up_bias_own,
        down_own.T,
        vec_own[7],
    )


def solution(mesh):
    both = P(("dp", "ctx"))
    in_specs = (
        P("dp", ("ctx", "tensor"), None),
        P("dp", "ctx", None),
        P("dp", None),
        both,
        both,
        P(None, ("dp", "ctx"), "tensor"),
        P(None, ("dp", "ctx")),
        P("tensor", ("dp", "ctx")),
        both,
        both,
        both,
        P(("dp", "ctx"), "tensor"),
        both,
        P("tensor", ("dp", "ctx")),
        both,
    )
    out_specs = (
        P("dp", ("ctx", "tensor"), None),
        P("dp", ("ctx", "tensor"), None),
        both,
        both,
        P(None, ("dp", "ctx"), "tensor"),
        P(None, ("dp", "ctx")),
        P("tensor", ("dp", "ctx")),
        both,
        both,
        both,
        P(("dp", "ctx"), "tensor"),
        both,
        P("tensor", ("dp", "ctx")),
        both,
    )
    return jax.shard_map(local, mesh=mesh, in_specs=in_specs, out_specs=out_specs, check_vma=False)
```

```python
import functools

import jax
import jax.numpy as jnp
from jax import lax
from jax.experimental import pallas as pl
from jax.experimental.pallas import tpu as pltpu
from jax.sharding import PartitionSpec as P

HEAD_DIM = 64
EPS = 1e-05
GELU_C = 0.7978845608028654
NEG = -1e30
TILE = 256
F32 = jnp.float32
BF16 = jnp.bfloat16


def layer_stats(rows):
    centred = rows - jnp.mean(rows, axis=-1, keepdims=True)
    inv_std = lax.rsqrt(jnp.mean(centred * centred, axis=-1, keepdims=True) + EPS)
    return (centred * inv_std, inv_std)


def norm_back(grad_out, normed, inv_std, gain):
    scaled = grad_out * gain
    return inv_std * (
        scaled
        - jnp.mean(scaled, axis=-1, keepdims=True)
        - normed * jnp.mean(scaled * normed, axis=-1, keepdims=True)
    )


def dot(left, right, dims=((1,), (0,))):
    return lax.dot_general(left, right, (dims, ((), ())), preferred_element_type=F32)


def causal_tile(size):
    key_row = lax.broadcasted_iota(jnp.int32, (size, size), 0)
    query_col = lax.broadcasted_iota(jnp.int32, (size, size), 1)
    return key_row <= query_col


def attend_kernel(dims, scalars, *refs):
    pieces, heads, shard, model, n_tokens, n_packed = dims
    token_parts, refs = refs[:n_tokens], refs[n_tokens:]
    packed_parts, refs = refs[:n_packed], refs[n_packed:]
    norm_one, vectors, heads_t, merge_t, q_pos, k_pos, v_pos, out_t, lse, attn = refs[:10]
    outs = refs[10:14]
    q_t, v_t, k_h, o_nat, tokens, packed, w_wide, w_low, merge, out = refs[14:]
    seq = pl.program_id(0)
    length, width = q_pos.shape
    rows = length // pieces
    blocks = length // TILE
    owners = packed.shape[0]
    first_slot = pl.num_programs(0) * pieces
    t_pos = scalars[first_slot + owners]
    place = 0
    for part in token_parts:
        tokens[place : place + part.shape[0], :] = part[...]
        place += part.shape[0]
    place = 0
    for part in packed_parts:
        packed[place : place + part.shape[0]] = part[...]
        place += part.shape[0]

    def tail_of(owner):
        return packed[scalars[first_slot + owner]].astype(F32)[shard:, :]

    def entry(tail, index):
        return tail[index : index + 1, :shard]

    tails = []
    for i in range(owners):
        block = packed[scalars[first_slot + i]].astype(F32)
        w_wide[i * shard : (i + 1) * shard, :] = block[:shard, :]
        tails.append(block[shard:, :])
    w_low[...] = w_wide[:, : 3 * width].astype(BF16)
    heads_t[...] = w_wide[:, : 3 * width].T.astype(BF16)
    merge_low = w_wide[:, 3 * width :]
    merge_t[...] = merge_low.astype(BF16)
    merge[...] = merge_low.T.astype(BF16)
    lines = [jnp.concatenate([entry(t, v) for t in tails], axis=1) for v in range(8)]
    group = width // shard
    mine = [tail_of(t_pos * group + k) for k in range(group)]
    bias_q = jnp.concatenate([entry(t, 2) for t in mine], axis=1)
    bias_v = jnp.concatenate([entry(t, 3) for t in mine], axis=1)
    long = model // width * shard
    bias_up = jnp.concatenate([t[8:9, model // 2 : model // 2 + long] for t in mine], axis=1)
    lines.append(bias_up)
    lines.append(jnp.zeros((16 - len(lines), model), F32))
    vectors[...] = jnp.concatenate(lines, axis=0)
    bias = jnp.concatenate([bias_q, jnp.zeros((1, width), F32), bias_v], axis=1)
    gain, shift = lines[0], lines[1]
    for p in range(pieces):
        first = pl.multiple_of(scalars[seq * pieces + p], rows)
        normed, unused = layer_stats(tokens[pl.ds(first, rows), :].astype(F32))
        normed = (normed * gain + shift).astype(BF16)
        norm_one[pl.ds(first, rows), :] = normed
        part = (dot(normed, w_low[...]) + bias).astype(BF16)
        here = slice(p * rows, (p + 1) * rows)
        q_pos[here, :] = part[:, :width] * jnp.asarray(HEAD_DIM ** (-0.5), BF16)
        k_pos[here, :] = part[:, width : 2 * width]
        v_pos[here, :] = part[:, 2 * width :]
    for b in range(blocks):
        here = slice(b * TILE, (b + 1) * TILE)
        q_t[:, here] = q_pos[here, :].T
        v_t[:, here] = v_pos[here, :].T
        key = k_pos[here, :]
        for h in range(heads):
            k_h[h, here, :] = key[:, h * HEAD_DIM : (h + 1) * HEAD_DIM]
    allowed = causal_tile(TILE)

    def one_head(h, unused):
        hs = pl.ds(pl.multiple_of(h * HEAD_DIM, HEAD_DIM), HEAD_DIM)
        for i in range(blocks):
            here = slice(i * TILE, (i + 1) * TILE)
            query = q_t[hs, here]
            diag = jnp.where(allowed, dot(k_h[h, here, :], query), NEG)
            top = jnp.max(diag, axis=0, keepdims=True)
            if i > 0:
                past = dot(k_h[h, : i * TILE, :], query)
                top = jnp.maximum(top, jnp.max(past, axis=0, keepdims=True))
            diag = jnp.exp(diag - top)
            total = jnp.sum(diag, axis=0, keepdims=True)
            mixed = dot(v_t[hs, here], diag.astype(BF16))
            if i > 0:
                past = jnp.exp(past - top)
                total += jnp.sum(past, axis=0, keepdims=True)
                mixed += dot(v_t[hs, : i * TILE], past.astype(BF16))
            out_t[hs, here] = mixed / total
            lse[h, :, here] = top + jnp.log(total)
        return unused

    lax.fori_loop(0, heads, one_head, 0)
    for b in range(blocks):
        here = slice(b * TILE, (b + 1) * TILE)
        o_nat[here, :] = out_t[:, here].T.astype(BF16)
    for p in range(pieces):
        first = pl.multiple_of(scalars[seq * pieces + p], rows)
        part = o_nat[p * rows : (p + 1) * rows, :]
        attn[pl.ds(first, rows), :] = part
        out[pl.ds(first, rows), :] = dot(part, merge[...]).astype(BF16)
    size = out.shape[0] // 4
    for j in range(4):
        outs[j][...] = out[j * size : (j + 1) * size, :]


def attend(scalars, token_parts, packed_parts, shard, width, seqs, pieces):
    total = sum(p.shape[0] for p in token_parts)
    model = token_parts[0].shape[1]
    owners = sum(p.shape[0] for p in packed_parts)
    heads = width // HEAD_DIM
    length = total // seqs
    nat = jax.ShapeDtypeStruct((seqs, length, width), BF16)
    nat_spec = pl.BlockSpec((None, length, width), lambda s, t: (s, 0, 0))
    pairs = heads * length * (length + TILE) // 2 * seqs
    whole = lambda *shape: pl.BlockSpec(shape, lambda s, t: (0,) * len(shape))
    return pl.pallas_call(
        functools.partial(
            attend_kernel, (pieces, heads, shard, model, len(token_parts), len(packed_parts))
        ),
        grid_spec=pltpu.PrefetchScalarGridSpec(
            num_scalar_prefetch=1,
            grid=(seqs,),
            in_specs=[whole(*p.shape) for p in token_parts + packed_parts],
            out_specs=[
                whole(total, model),
                whole(16, model),
                whole(3 * width, model),
                whole(model, width),
                nat_spec,
                nat_spec,
                nat_spec,
                pl.BlockSpec((None, width, length), lambda s, t: (s, 0, 0)),
                pl.BlockSpec((None, heads, 1, length), lambda s, t: (s, 0, 0, 0)),
                whole(total, width),
            ]
            + [whole(total // 4, model)] * 4,
            scratch_shapes=[
                pltpu.VMEM((width, length), BF16),
                pltpu.VMEM((width, length), BF16),
                pltpu.VMEM((heads, length, HEAD_DIM), BF16),
                pltpu.VMEM((length, width), BF16),
                pltpu.VMEM((total, model), BF16),
                pltpu.VMEM((owners,) + packed_parts[0].shape[1:], BF16),
                pltpu.VMEM((model, 4 * width), F32),
                pltpu.VMEM((model, 3 * width), BF16),
                pltpu.VMEM((width, model), BF16),
                pltpu.VMEM((total, model), BF16),
            ],
        ),
        out_shape=[
            jax.ShapeDtypeStruct((total, model), BF16),
            jax.ShapeDtypeStruct((16, model), F32),
            jax.ShapeDtypeStruct((3 * width, model), BF16),
            jax.ShapeDtypeStruct((model, width), BF16),
            nat,
            nat,
            nat,
            jax.ShapeDtypeStruct((seqs, width, length), F32),
            jax.ShapeDtypeStruct((seqs, heads, 1, length), F32),
            jax.ShapeDtypeStruct((total, width), BF16),
        ]
        + [jax.ShapeDtypeStruct((total // 4, model), BF16)] * 4,
        compiler_params=pltpu.CompilerParams(vmem_limit_bytes=58 * 2**20),
        cost_estimate=pl.CostEstimate(
            flops=32 * HEAD_DIM * pairs, bytes_accessed=24 * total * model, transcendentals=pairs
        ),
        name="attend",
    )(scalars, *token_parts, *packed_parts)


def attend_back_kernel(dims, starts, *refs):
    pieces, heads, shard, ctx, t_index = dims
    row_parts, refs = refs[:4], refs[4:]
    merge_t, heads_t, norm_one, attn, q_pos, k_pos, v_pos, out_t, lse = refs[:9]
    vectors, resid_sums = refs[9:11]
    up_sums, backs, weights = refs[11:15], refs[15:19], refs[19]
    grad_rows, do_nat, q_t, k_t, do_t, q_h, k_h, v_h, do_h, row_dot, dq_t, dk_h, dv_h, g_nat = (
        refs[20:34]
    )
    g_t, back, w_full, p_low, s_low = refs[34:]
    t_pos = starts[t_index]
    seq = pl.program_id(0)
    length, width = q_pos.shape
    model = norm_one.shape[1]
    rows = length // pieces
    blocks = length // TILE
    place = 0
    for part in row_parts:
        grad_rows[place : place + part.shape[0], :] = part[...]
        place += part.shape[0]
    for p in range(pieces):
        first = pl.multiple_of(starts[seq * pieces + p], rows)
        part = dot(grad_rows[pl.ds(first, rows), :], merge_t[...])
        do_nat[p * rows : (p + 1) * rows, :] = part.astype(BF16)
    for b in range(blocks):
        here = slice(b * TILE, (b + 1) * TILE)
        query, key, value, grad = q_pos[here, :], k_pos[here, :], v_pos[here, :], do_nat[here, :]
        q_t[:, here] = query.T
        k_t[:, here] = key.T
        grad_t = grad.T
        do_t[:, here] = grad_t
        product = grad_t.astype(F32) * out_t[:, here]
        for h in range(heads):
            cols = slice(h * HEAD_DIM, (h + 1) * HEAD_DIM)
            q_h[h, here, :] = query[:, cols]
            k_h[h, here, :] = key[:, cols]
            v_h[h, here, :] = value[:, cols]
            do_h[h, here, :] = grad[:, cols]
            row_dot[h, :, here] = jnp.sum(product[cols, :], axis=0, keepdims=True)
    allowed = causal_tile(TILE)

    def one_head(h, unused):
        hs = pl.ds(pl.multiple_of(h * HEAD_DIM, HEAD_DIM), HEAD_DIM)
        for j in range(blocks):
            here = slice(j * TILE, (j + 1) * TILE)
            key, value = k_h[h, here, :], v_h[h, here, :]
            key_t = k_t[hs, here]
            for i in range(j, blocks):
                cols = slice(i * TILE, (i + 1) * TILE)
                scores = dot(key, q_t[hs, cols])
                if i == j:
                    scores = jnp.where(allowed, scores, NEG)
                probs = jnp.exp(scores - lse[h, :, cols])
                slope = probs * (dot(value, do_t[hs, cols]) - row_dot[h, :, cols])
                p_low[:, cols] = probs.astype(BF16)
                s_low[:, cols] = slope.astype(BF16)
            later = slice(j * TILE, length)
            grad_v = dot(p_low[:, later], do_h[h, later, :])
            grad_k = dot(s_low[:, later], q_h[h, later, :])
            add = dot(key_t, s_low[:, later])
            dq_t[hs, later] = add if j == 0 else dq_t[hs, later] + add
            dk_h[h, here, :] = grad_k
            dv_h[h, here, :] = grad_v
        return unused

    lax.fori_loop(0, heads, one_head, 0)
    wide = jnp.zeros((1, 3 * width), F32)
    for b in range(blocks):
        here = slice(b * TILE, (b + 1) * TILE)
        grad_q = dq_t[:, here].T * (HEAD_DIM ** (-0.5))
        grad_k = jnp.concatenate([dk_h[h, here, :] for h in range(heads)], axis=1)
        grad_v = jnp.concatenate([dv_h[h, here, :] for h in range(heads)], axis=1)
        grads = jnp.concatenate([grad_q, grad_k, grad_v], axis=1)
        wide += jnp.sum(grads, axis=0, keepdims=True)
        g_nat[here, :] = grads.astype(BF16)
    w_t = jnp.zeros((3 * width, model), F32)
    m_t = jnp.zeros((width, model), F32)
    column = jnp.zeros((3 * width, 1), F32)
    for p in range(pieces):
        first = pl.multiple_of(starts[seq * pieces + p], rows)
        part = g_nat[p * rows : (p + 1) * rows, :]
        back[pl.ds(first, rows), :] = dot(part, heads_t[...]).astype(BF16)
    for p in range(pieces):
        first = pl.multiple_of(starts[seq * pieces + p], rows)
        g_t[:, :] = g_nat[p * rows : (p + 1) * rows, :].astype(F32).T
        turned = g_t[...]
        column += jnp.sum(turned, axis=1, keepdims=True)
        w_t += dot(turned.astype(BF16), norm_one[pl.ds(first, rows), :])
        mine = attn[pl.ds(first, rows), :].astype(F32).T.astype(BF16)
        m_t += dot(mine, grad_rows[pl.ds(first, rows), :])
    w_full[:, : 3 * width] = w_t.T
    w_full[:, 3 * width :] = m_t.T
    size = back.shape[0] // 4
    for j in range(4):
        backs[j][...] = back[j * size : (j + 1) * size, :]
    factor = heads_t[...].astype(F32)
    group = lax.broadcasted_iota(jnp.int32, (1, model), 1) // width
    spread = lambda part: jnp.where(
        group == t_pos, jnp.concatenate([part] * (model // width), axis=1), 0.0
    )
    shift_sum = jnp.sum(factor * column, axis=0, keepdims=True)
    gain_sum = jnp.sum(factor * w_t, axis=0, keepdims=True) - vectors[1:2, :] * shift_sum
    up_sum = up_sums[0][...] + up_sums[1][...] + up_sums[2][...] + up_sums[3][...]
    lines = jnp.concatenate(
        [
            gain_sum / vectors[0:1, :],
            shift_sum,
            spread(wide[:, :width]),
            spread(wide[:, 2 * width :]),
            resid_sums[0:4, :],
        ],
        axis=0,
    )
    owners = model // shard
    long = model // width * shard
    for i in range(owners):
        k, lane = i * long // model, i * long % model
        here = slice(i * shard, (i + 1) * shard)
        block = [
            w_full[here, :],
            jnp.concatenate([lines[:, here], jnp.zeros((8, model - shard), F32)], axis=1),
            jnp.concatenate(
                [
                    jnp.where(t_pos == k, up_sum[:, lane : lane + long], 0.0),
                    jnp.zeros((1, model - long), F32),
                ],
                axis=1,
            ),
            jnp.zeros((7, model), F32),
        ]
        weights[i % ctx, i // ctx] = jnp.concatenate(block, axis=0).astype(BF16)


def attend_back(starts, row_parts, merge_t, heads_t, norm_one, attn, kept, lines, shard, ctx, pieces):
    q_pos, k_pos, v_pos, out_t, lse = kept
    total, model = norm_one.shape
    width = merge_t.shape[1]
    seqs, length, unused = q_pos.shape
    heads = width // HEAD_DIM
    nat_spec = pl.BlockSpec((None, length, width), lambda s, t: (s, 0, 0))
    whole = lambda *shape: pl.BlockSpec(shape, lambda s, t: (0,) * len(shape))
    pairs = heads * length * (length + TILE) // 2 * seqs
    per_head = pltpu.VMEM((heads, length, HEAD_DIM), BF16)
    by_owner = (ctx, model // shard // ctx, shard + 16, 4 * width)
    across = pltpu.VMEM((width, length), BF16)
    return pl.pallas_call(
        functools.partial(
            attend_back_kernel, (pieces, heads, shard, ctx, starts.shape[0] - 1)
        ),
        grid_spec=pltpu.PrefetchScalarGridSpec(
            num_scalar_prefetch=1,
            grid=(seqs,),
            in_specs=[whole(*p.shape) for p in row_parts]
            + [
                whole(model, width),
                whole(3 * width, model),
                whole(total, model),
                whole(total, width),
                nat_spec,
                nat_spec,
                nat_spec,
                pl.BlockSpec((None, width, length), lambda s, t: (s, 0, 0)),
                pl.BlockSpec((None, heads, 1, length), lambda s, t: (s, 0, 0, 0)),
            ]
            + [whole(*v.shape) for v in lines],
            out_specs=[whole(total // 4, model)] * 4
            + [
                pl.BlockSpec((None,) + by_owner, lambda s, t: (s, 0, 0, 0, 0)),
            ],
            scratch_shapes=[
                pltpu.VMEM((total, model), BF16),
                pltpu.VMEM((length, width), BF16),
                across,
                across,
                across,
                per_head,
                per_head,
                per_head,
                per_head,
                pltpu.VMEM((heads, 1, length), F32),
                pltpu.VMEM((width, length), F32),
                pltpu.VMEM((heads, length, HEAD_DIM), F32),
                pltpu.VMEM((heads, length, HEAD_DIM), F32),
                pltpu.VMEM((length, 3 * width), BF16),
                pltpu.VMEM((3 * width, length // pieces), F32),
                pltpu.VMEM((total, model), BF16),
                pltpu.VMEM((model, 4 * width), F32),
                pltpu.VMEM((TILE, length), BF16),
                pltpu.VMEM((TILE, length), BF16),
            ],
        ),
        out_shape=[jax.ShapeDtypeStruct((total // 4, model), BF16)] * 4
        + [
            jax.ShapeDtypeStruct((seqs,) + by_owner, BF16),
        ],
        compiler_params=pltpu.CompilerParams(vmem_limit_bytes=60 * 2**20),
        cost_estimate=pl.CostEstimate(
            flops=60 * HEAD_DIM * pairs, bytes_accessed=24 * total * model, transcendentals=pairs
        ),
        name="attend_back",
    )(starts, *row_parts, merge_t, heads_t, norm_one, attn, q_pos, k_pos, v_pos, out_t, lse, *lines)


def feed_kernel(
    seqs,
    ctx,
    table,
    norm,
    g_own,
    g_far,
    up,
    down_t,
    bias,
    act,
    pre_low,
    back,
    g_out,
    sums,
):
    step = pl.program_id(0)
    distance = lax.rem(lax.div(step, seqs), ctx)
    grad = jnp.where(distance == 0, g_own[...], g_far[...])
    g_out[...] = grad
    pre = dot(norm[...], up[...]) + bias[...]
    grad_act = dot(grad, down_t[...])
    square = pre * pre
    tangent = jnp.tanh(GELU_C * (pre + 0.044715 * square * pre))
    half = 0.5 * (1.0 + tangent)
    low_act = (pre * half).astype(BF16)
    act[...] = low_act
    slope = half + 0.5 * pre * (1.0 - tangent * tangent) * (
        GELU_C + (GELU_C * 3.0 * 0.044715) * square
    )
    grad_pre = grad_act * slope
    total = jnp.sum(grad_pre, axis=0, keepdims=True)
    sums[...] = jnp.where(step == 0, total, sums[...] + total)
    low = grad_pre.astype(BF16)
    pre_low[...] = low
    back[...] = dot(low, up[...], ((1,), (1,))).astype(BF16)


def feed(table, norm, g_own, g_far, second, bias, seqs, ctx, limit):
    total, model = norm.shape
    rows = g_own.shape[1]
    hidden = second.shape[1] // 2
    steps = total // rows
    by_rows = lambda size: pl.BlockSpec((rows, size), lambda i, t: (i, 0))
    return pl.pallas_call(
        functools.partial(feed_kernel, seqs, ctx),
        grid_spec=pltpu.PrefetchScalarGridSpec(
            num_scalar_prefetch=1,
            grid=(steps,),
            in_specs=[
                by_rows(model),
                pl.BlockSpec((None, rows, model), lambda i, t: (t[i], 0, 0)),
                pl.BlockSpec((None, rows, model), lambda i, t: (t[steps + i], 0, 0)),
                pl.BlockSpec((model, hidden), lambda i, t: (0, 0)),
                pl.BlockSpec((model, hidden), lambda i, t: (0, 1)),
                pl.BlockSpec((1, hidden), lambda i, t: (0, 0)),
            ],
            out_specs=[
                by_rows(hidden),
                by_rows(hidden),
                by_rows(model),
                by_rows(model),
                pl.BlockSpec((1, hidden), lambda i, t: (0, 0)),
            ],
        ),
        out_shape=[
            jax.ShapeDtypeStruct((total, hidden), BF16),
            jax.ShapeDtypeStruct((total, hidden), BF16),
            jax.ShapeDtypeStruct((total, model), BF16),
            jax.ShapeDtypeStruct((total, model), BF16),
            jax.ShapeDtypeStruct((1, hidden), F32),
        ],
        compiler_params=pltpu.CompilerParams(vmem_limit_bytes=limit * 2**20),
        cost_estimate=pl.CostEstimate(
            flops=6 * total * model * hidden,
            bytes_accessed=14 * total * model,
            transcendentals=total * hidden,
        ),
        name="feed",
    )(table, norm, g_own, g_far, second, second, bias)


def resid_kernel(own, beside, across, resid, grad, vectors, out, low, sums):
    step = pl.program_id(0)
    normed, inv_std = layer_stats(resid[...])
    back = own[...].astype(F32) + beside[...].astype(F32) + across[...].astype(F32)
    given = grad[...].astype(F32)
    total = given + norm_back(back, normed, inv_std, vectors[5:6, :])
    out[...] = total
    low[...] = total.astype(BF16)
    add = lambda rows: jnp.sum(rows, axis=0, keepdims=True)
    lines = jnp.concatenate(
        [add(total), add(back * normed), add(back), add(given), jnp.zeros((4, total.shape[1]), F32)],
        axis=0,
    )
    sums[...] = jnp.where(step == 0, lines, sums[...] + lines)


def first_kernel(own, beside, across, rows, grad, vectors, out, low):
    normed, inv_std = layer_stats(rows[...].astype(F32))
    back = own[...].astype(F32) + beside[...].astype(F32) + across[...].astype(F32)
    total = grad[...] + norm_back(back, normed, inv_std, vectors[0:1, :])
    out[...] = total
    low[...] = total.astype(BF16)


def row_wise(kernel, parts, vectors, with_sums):
    total, model = parts[3].shape
    steps = 1
    by_rows = pl.BlockSpec((total // steps, model), lambda i: (i, 0))
    fixed = lambda rows: pl.BlockSpec((rows, model), lambda i: (0, 0))
    return pl.pallas_call(
        kernel,
        grid=(steps,),
        in_specs=[by_rows] * len(parts) + [fixed(16)],
        out_specs=[by_rows, by_rows] + [fixed(8)] * with_sums,
        out_shape=[
            jax.ShapeDtypeStruct((total, model), F32),
            jax.ShapeDtypeStruct((total, model), BF16),
        ]
        + [jax.ShapeDtypeStruct((8, model), F32)] * with_sums,
        cost_estimate=pl.CostEstimate(
            flops=20 * total * model, bytes_accessed=18 * total * model, transcendentals=total
        ),
        compiler_params=pltpu.CompilerParams(vmem_limit_bytes=40 * 2**20),
        name="row_wise",
    )(*parts, vectors)


def heads_kernel(width, a, b, c, d, heads, merge, small):
    shard = merge.shape[1]
    total = sum(part[...].astype(F32) for part in (a, b, c, d))
    for m in range(3):
        heads[m] = total[:shard, m * width : (m + 1) * width]
    merge[...] = total[:shard, 3 * width :].T
    small[...] = total[shard:, :]


def finish_heads(parts, width):
    shard = parts[0].shape[0] - 16
    if len(parts) != 4:
        low = [sum(p.astype(F32) for p in parts)] + [jnp.zeros(parts[0].shape, F32)] * 3
        parts = low
    return pl.pallas_call(
        functools.partial(heads_kernel, width),
        out_shape=[
            jax.ShapeDtypeStruct((3, shard, width), F32),
            jax.ShapeDtypeStruct((width, shard), F32),
            jax.ShapeDtypeStruct((16, 4 * width), F32),
        ],
        name="finish_heads",
    )(*parts)


def swap_tensor(block, bit):
    size = lax.axis_size("tensor")
    return lax.ppermute(block, "tensor", [(i, i ^ bit) for i in range(size)])


def rotate(block, axis, distance):
    size = lax.axis_size(axis)
    return lax.ppermute(block, axis, [(i, (i + distance) % size) for i in range(size)])


def scatter_tensor(parts):
    far = swap_tensor(parts[3], 1)
    near = (parts[2].astype(F32) + far.astype(F32)).astype(BF16)
    across = swap_tensor(near, 2)
    beside = swap_tensor(parts[1], 1)
    return (parts[0], beside, across)


def quarters(rows):
    size = rows.shape[0] // 4
    return [rows[j * size : (j + 1) * size] for j in range(4)]


def add_all(parts):
    return sum(p.astype(F32) for p in parts)


def pick(array, index):
    return lax.dynamic_index_in_dim(array, index, 0, keepdims=False)


def scatter_ctx(blocks):
    ctx, ctx_pos = lax.axis_size("ctx"), lax.axis_index("ctx")
    take = lambda c: lax.dynamic_index_in_dim(blocks, c, 1, keepdims=False)
    total = take(ctx_pos).astype(F32)
    for d in range(1, ctx):
        total += rotate(take((ctx_pos + d) % ctx), "ctx", d).astype(F32)
    return total.astype(BF16)


def scatter_dp(blocks, before_last=None):
    dp, dp_pos = lax.axis_size("dp"), lax.axis_index("dp")
    parts = [pick(blocks, (dp_pos + d) % dp) for d in range(dp)]
    if before_last is not None:
        parts[-1], unused = lax.optimization_barrier((parts[-1], before_last))
    return parts[:1] + [rotate(parts[d], "dp", d) for d in range(1, dp)]


def local(
    tokens,
    cotangent,
    stretch_order,
    attn_gain,
    attn_shift,
    heads_weight,
    heads_bias,
    merge_weight,
    merge_bias,
    feed_gain,
    feed_shift,
    up_weight,
    up_bias,
    down_weight,
    down_bias,
):
    t_size, t_pos = lax.axis_size("tensor"), lax.axis_index("tensor")
    c_size, c_pos = lax.axis_size("ctx"), lax.axis_index("ctx")
    dp_size, dp_pos = lax.axis_size("dp"), lax.axis_index("dp")
    owners = dp_size * c_size
    seqs_in, rows, model = tokens.shape
    seqs = seqs_in // c_size
    shard = heads_weight.shape[1]
    width = heads_weight.shape[2]
    hidden = up_weight.shape[1]
    hidden_all = hidden * t_size
    pieces = c_size * t_size
    span_rows = c_size * seqs * rows

    by_owner = tokens.reshape(c_size, seqs, rows, model)
    near = pick(by_owner, c_pos).reshape(-1, model)
    far = [rotate(pick(by_owner, (c_pos - d) % c_size), "ctx", -d) for d in range(1, c_size)]
    far = jnp.concatenate(far, axis=0).reshape(-1, model)
    near_x = swap_tensor(near, 2)
    far_x = swap_tensor(far, 2)
    own_rows = jnp.concatenate([near, far], axis=0)

    line = lax.broadcasted_iota(jnp.int32, (16, shard), 0)
    small = jnp.zeros((16, shard), BF16)
    for index, vector in enumerate(
        [
            attn_gain[None],
            attn_shift[None],
            heads_bias[0:1],
            heads_bias[1:2],
            merge_bias[None],
            feed_gain[None],
            feed_shift[None],
            down_bias[None],
        ]
    ):
        small = jnp.where(line == index, vector, small)
    up_size = up_bias.shape[0]
    up_line = jnp.where(
        lax.broadcasted_iota(jnp.int32, (16, up_size), 0) == 8, up_bias[None], jnp.zeros((), BF16)
    )
    gap = lambda size: jnp.zeros((16, size), BF16)
    tail = [small, gap(model // 2 - shard), up_line]
    if model // 2 > up_size:
        tail.append(gap(model // 2 - up_size))
    first_pack = jnp.concatenate(
        [
            jnp.concatenate(
                [heads_weight[0], heads_weight[1], heads_weight[2], merge_weight.T], axis=1
            ),
            jnp.concatenate(tail, axis=1),
        ],
        axis=0,
    )
    by_dp = [first_pack] + [rotate(first_pack, "dp", -d) for d in range(1, dp_size)]
    packed_parts = by_dp + [rotate(p, "ctx", -d) for d in range(1, c_size) for p in by_dp]
    second_pack = jnp.concatenate([up_weight, down_weight.T], axis=1)
    second_pack, by_dp[-1] = lax.optimization_barrier((second_pack, by_dp[-1]))
    packed_parts = [p[None] for p in packed_parts]
    second_all = lax.all_gather(second_pack, ("dp", "ctx"), axis=0, tiled=True)

    near_1, far_1 = swap_tensor(near, 1), swap_tensor(far, 1)
    near_3, far_3 = swap_tensor(near_x, 1), swap_tensor(far_x, 1)
    token_parts = [near, far, near_1, far_1, near_x, far_x, near_3, far_3]

    per_stretch = t_size // 2
    order = lax.dynamic_slice_in_dim(stretch_order, c_pos * seqs, seqs, 0)
    stretches = order.shape[1]
    span = jnp.arange(stretches, dtype=jnp.int32)
    inverse = jnp.sum(
        jnp.where(order[:, :, None] == span[None, None, :], span[None, :, None], 0), axis=1
    )
    stored = inverse[:, :, None]
    part = jnp.arange(per_stretch, dtype=jnp.int32)[None, None, :]
    slot = ((stored % 2) * per_stretch + part) ^ t_pos
    away = (stored // 2 - c_pos) % c_size
    seq_id = jnp.arange(seqs, dtype=jnp.int32)[:, None, None]
    starts = (((slot * c_size + away) * seqs + seq_id) * rows).reshape(-1)
    owner = jnp.arange(owners, dtype=jnp.int32)
    slots = ((owner % c_size - c_pos) % c_size) * dp_size + (owner // c_size - dp_pos) % dp_size
    scalars = jnp.concatenate([starts, slots, t_pos[None].astype(jnp.int32)])

    g_blocks = cotangent.reshape(c_size, seqs, 2, t_size // 2, rows, model)
    bit = t_pos % 2
    g_moved = [
        rotate(
            lax.dynamic_index_in_dim(pick(g_blocks, (c_pos - d) % c_size), bit, 1, keepdims=False),
            "ctx",
            -d,
        )
        for d in range(1, c_size)
    ]
    g_moved = jnp.stack(g_moved)

    norm_one, vec, heads_t, merge_t, q_pos, k_pos, v_pos, out_t, lse, attn, *shares = attend(
        scalars, token_parts, packed_parts, shard, width, seqs, pieces
    )
    shares[3], g_moved = lax.optimization_barrier((shares[3], g_moved))
    merged = add_all(scatter_tensor(shares))
    b_merge, gain_two, shift_two, b_down = vec[4], vec[5], vec[6], vec[7]
    rows_in = own_rows.astype(F32)
    resid = rows_in + merged + b_merge

    normed_two, inv_two = layer_stats(resid)
    norm_0 = (normed_two * gain_two + shift_two).astype(BF16)
    norm_2 = swap_tensor(norm_0, 2)
    norm_1 = swap_tensor(norm_0, 1)
    g_own = cotangent.reshape(-1, rows, model)
    g_far = jnp.stack([g_moved, swap_tensor(g_moved, 1)], axis=2).reshape(-1, rows, model)
    b_up = vec[8:9, :hidden]

    def feed_part(offsets, norm, limit):
        own_table, far_table = [], []
        for j in offsets:
            piece = t_pos ^ j
            for d in range(c_size):
                for q in range(seqs):
                    own_table.append((c_pos * seqs + q) * t_size + piece if d == 0 else 0 * piece)
                    place = (piece // 2) ^ bit
                    far_row = (((d - 1) * seqs + q) * 2 + place) * (t_size // 2) + piece % 2
                    far_table.append(far_row if d > 0 else 0 * piece)
        table = jnp.stack(own_table + far_table).astype(jnp.int32)
        return feed(table, norm, g_own, g_far, second_all, b_up, seqs, c_size, limit)

    act_0, pre_0, back_0, g_0, up_sum_0 = feed_part((0,), norm_0, 60)
    act_1, pre_1, back_1, g_1, up_sum_1 = feed_part((1,), norm_1, 60)
    norm_2, up_sum_0, up_sum_1 = lax.optimization_barrier((norm_2, up_sum_0, up_sum_1))
    norm_3 = swap_tensor(norm_2, 1)
    act_3, pre_3, back_3, g_3, up_sum_3 = feed_part((3,), norm_3, 20)
    act_2, pre_2, back_2, g_2, up_sum_2 = feed_part((2,), norm_2, 20)
    unused, beside, across = scatter_tensor([back_0, back_1, back_2, back_3])

    together = lambda *parts: jnp.concatenate(parts, axis=0)
    norm_all = together(norm_0, norm_1, norm_2, norm_3)
    grad_all = together(g_0, g_1, g_2, g_3)
    grad_down_t = dot(grad_all, together(act_0, act_1, act_2, act_3), ((0,), (0,)))
    grad_up = dot(norm_all, together(pre_0, pre_1, pre_2, pre_3), ((0,), (0,)))
    by_place = lambda grad: grad.astype(BF16).reshape(dp_size, c_size, shard, hidden)
    grad_down_t, grad_up = by_place(grad_down_t), by_place(grad_up)
    down_half = scatter_ctx(grad_down_t)
    across, down_half, grad_up = lax.optimization_barrier((across, down_half, grad_up))
    feed_half = jnp.stack([scatter_ctx(grad_up), down_half], axis=1)
    grad_resid, resid_0, resid_sums = row_wise(
        resid_kernel, [back_0, beside, across, resid, g_0], vec, True
    )
    resid_2 = swap_tensor(resid_0, 2)
    resid_1 = swap_tensor(resid_0, 1)
    w_down = second_all[:, hidden:].T
    mix_0, mix_1, mix_2, mix_3 = (
        dot(a, w_down).astype(BF16) for a in (act_0, act_1, act_2, act_3)
    )
    mix_near = (mix_2.astype(F32) + swap_tensor(mix_3, 1).astype(F32)).astype(BF16)
    resid_2, mix_near, mix_0, mix_1, unused = lax.optimization_barrier(
        (resid_2, mix_near, mix_0, mix_1, feed_half[0, 0, :8, :128])
    )
    mix_across = swap_tensor(mix_near, 2)
    feed_parts = scatter_dp(feed_half)

    *backs, weights = attend_back(
        scalars,
        [resid_0, resid_1, resid_2, swap_tensor(resid_2, 1)],
        merge_t,
        heads_t,
        norm_one,
        attn,
        (q_pos, k_pos, v_pos, out_t, lse),
        [vec, resid_sums, up_sum_0, up_sum_1, up_sum_2, up_sum_3],
        shard,
        c_size,
        pieces,
    )
    weights, feed_parts, mix_across, mix_1, backs[1], backs[3] = lax.optimization_barrier(
        (weights, feed_parts, mix_across, mix_1, backs[1], backs[3])
    )
    mix_beside = swap_tensor(mix_1, 1)
    near = (backs[2].astype(F32) + swap_tensor(backs[3], 1).astype(F32)).astype(BF16)
    weights, near = lax.optimization_barrier((weights, near))
    across, beside = swap_tensor(near, 2), swap_tensor(backs[1], 1)
    if seqs == 1:
        weights = weights[0]
    else:
        weights = jnp.sum(weights.astype(F32), axis=0).astype(BF16)
    heads_half = pick(weights, c_pos).astype(F32)
    for d in range(1, c_size):
        heads_half += rotate(pick(weights, (c_pos + d) % c_size), "ctx", d).astype(F32)
    heads_half = heads_ctx = heads_half.astype(BF16)
    heads_parts = scatter_dp(heads_half, across)
    feed_parts, unused = lax.optimization_barrier((feed_parts, across))
    feed_own = add_all(feed_parts)
    up_own, down_own = feed_own[0], feed_own[1]
    mixed = add_all([mix_0, mix_beside, mix_across])
    block_rows = (resid + mixed + b_down).astype(BF16)

    def send_back(low, own):
        parts = low.reshape(c_size, seqs, rows, model)
        held = jnp.stack(
            [own.reshape(c_size, seqs, rows, model)[0]]
            + [rotate(parts[d], "ctx", d).astype(own.dtype) for d in range(1, c_size)]
        )
        return jnp.concatenate(
            [pick(held, (c_pos - s) % c_size) for s in range(c_size)], axis=0
        )

    block_rows, unused = lax.optimization_barrier((block_rows, heads_ctx))
    block_out = send_back(block_rows, block_rows)
    tokens_rows, tokens_low = row_wise(
        first_kernel, [backs[0], beside, across, own_rows, grad_resid], vec, False
    )
    tokens_grad = send_back(tokens_low, tokens_rows)
    heads_parts, unused = lax.optimization_barrier((heads_parts, block_out))
    heads_own, merge_own, sums = finish_heads(heads_parts, width)

    sums = add_all([sums] + [rotate(sums, "tensor", d) for d in range(1, t_size)])
    vec_own = sums[:8, :shard]
    up_bias_own = sums[8, : hidden_all // owners]
    return (
        block_out,
        tokens_grad,
        vec_own[0],
        vec_own[1],
        heads_own,
        vec_own[2:4],
        merge_own,
        vec_own[4],
        vec_own[5],
        vec_own[6],
        up_own,
        up_bias_own,
        down_own.T,
        vec_own[7],
    )


def solution(mesh):
    both = P(("dp", "ctx"))
    in_specs = (
        P("dp", ("ctx", "tensor"), None),
        P("dp", "ctx", None),
        P("dp", None),
        both,
        both,
        P(None, ("dp", "ctx"), "tensor"),
        P(None, ("dp", "ctx")),
        P("tensor", ("dp", "ctx")),
        both,
        both,
        both,
        P(("dp", "ctx"), "tensor"),
        both,
        P("tensor", ("dp", "ctx")),
        both,
    )
    out_specs = (
        P("dp", ("ctx", "tensor"), None),
        P("dp", ("ctx", "tensor"), None),
        both,
        both,
        P(None, ("dp", "ctx"), "tensor"),
        P(None, ("dp", "ctx")),
        P("tensor", ("dp", "ctx")),
        both,
        both,
        both,
        P(("dp", "ctx"), "tensor"),
        both,
        P("tensor", ("dp", "ctx")),
        both,
    )
    return jax.shard_map(local, mesh=mesh, in_specs=in_specs, out_specs=out_specs, check_vma=False)
```

```python
import functools

import jax
import jax.numpy as jnp
from jax import lax
from jax.experimental import pallas as pl
from jax.experimental.pallas import tpu as pltpu
from jax.sharding import PartitionSpec as P

HEAD_DIM = 64
EPS = 1e-05
GELU_C = 0.7978845608028654
NEG = -1e30
TILE = 256
F32 = jnp.float32
BF16 = jnp.bfloat16


def layer_stats(rows):
    centred = rows - jnp.mean(rows, axis=-1, keepdims=True)
    inv_std = lax.rsqrt(jnp.mean(centred * centred, axis=-1, keepdims=True) + EPS)
    return (centred * inv_std, inv_std)


def norm_back(grad_out, normed, inv_std, gain):
    scaled = grad_out * gain
    return inv_std * (
        scaled
        - jnp.mean(scaled, axis=-1, keepdims=True)
        - normed * jnp.mean(scaled * normed, axis=-1, keepdims=True)
    )


def dot(left, right, dims=((1,), (0,))):
    return lax.dot_general(left, right, (dims, ((), ())), preferred_element_type=F32)


def causal_tile(size):
    key_row = lax.broadcasted_iota(jnp.int32, (size, size), 0)
    query_col = lax.broadcasted_iota(jnp.int32, (size, size), 1)
    return key_row <= query_col


def attend_kernel(dims, scalars, *refs):
    pieces, heads, shard, model, n_tokens, n_packed = dims
    token_parts, refs = refs[:n_tokens], refs[n_tokens:]
    packed_parts, refs = refs[:n_packed], refs[n_packed:]
    norm_one, vectors, heads_t, merge_t, q_pos, k_pos, v_pos, out_t, lse, attn = refs[:10]
    outs = refs[10:14]
    q_t, v_t, k_h, o_nat, tokens, packed, w_wide, w_low, merge, out, s_wide, p_low = refs[14:]
    seq = pl.program_id(0)
    length, width = q_pos.shape
    rows = length // pieces
    blocks = length // TILE
    owners = packed.shape[0]
    first_slot = pl.num_programs(0) * pieces
    t_pos = scalars[first_slot + owners]
    place = 0
    for part in token_parts:
        tokens[place : place + part.shape[0], :] = part[...]
        place += part.shape[0]
    place = 0
    for part in packed_parts:
        packed[place : place + part.shape[0]] = part[...]
        place += part.shape[0]

    def tail_of(owner):
        return packed[scalars[first_slot + owner]].astype(F32)[shard:, :]

    def entry(tail, index):
        return tail[index : index + 1, :shard]

    tails = []
    for i in range(owners):
        block = packed[scalars[first_slot + i]].astype(F32)
        w_wide[i * shard : (i + 1) * shard, :] = block[:shard, :]
        tails.append(block[shard:, :])
    w_low[...] = w_wide[:, : 3 * width].astype(BF16)
    heads_t[...] = w_wide[:, : 3 * width].T.astype(BF16)
    merge_low = w_wide[:, 3 * width :]
    merge_t[...] = merge_low.astype(BF16)
    merge[...] = merge_low.T.astype(BF16)
    lines = [jnp.concatenate([entry(t, v) for t in tails], axis=1) for v in range(8)]
    group = width // shard
    mine = [tail_of(t_pos * group + k) for k in range(group)]
    bias_q = jnp.concatenate([entry(t, 2) for t in mine], axis=1)
    bias_v = jnp.concatenate([entry(t, 3) for t in mine], axis=1)
    long = model // width * shard
    bias_up = jnp.concatenate([t[8:9, model // 2 : model // 2 + long] for t in mine], axis=1)
    lines.append(bias_up)
    lines.append(jnp.zeros((16 - len(lines), model), F32))
    vectors[...] = jnp.concatenate(lines, axis=0)
    bias = jnp.concatenate([bias_q, jnp.zeros((1, width), F32), bias_v], axis=1)
    gain, shift = lines[0], lines[1]
    for p in range(pieces):
        first = pl.multiple_of(scalars[seq * pieces + p], rows)
        normed, unused = layer_stats(tokens[pl.ds(first, rows), :].astype(F32))
        normed = (normed * gain + shift).astype(BF16)
        norm_one[pl.ds(first, rows), :] = normed
        part = (dot(normed, w_low[...]) + bias).astype(BF16)
        here = slice(p * rows, (p + 1) * rows)
        q_pos[here, :] = part[:, :width] * jnp.asarray(HEAD_DIM ** (-0.5), BF16)
        k_pos[here, :] = part[:, width : 2 * width]
        v_pos[here, :] = part[:, 2 * width :]
    for b in range(blocks):
        here = slice(b * TILE, (b + 1) * TILE)
        q_t[:, here] = q_pos[here, :].T
        v_t[:, here] = v_pos[here, :].T
        key = k_pos[here, :]
        for h in range(heads):
            k_h[h, here, :] = key[:, h * HEAD_DIM : (h + 1) * HEAD_DIM]
    allowed = causal_tile(TILE)

    def one_head(h, unused):
        hs = pl.ds(pl.multiple_of(h * HEAD_DIM, HEAD_DIM), HEAD_DIM)
        for i in range(blocks):
            here = slice(i * TILE, (i + 1) * TILE)
            query = q_t[hs, here]
            tops = None
            for j in range(i + 1):
                scores = dot(k_h[h, j * TILE : (j + 1) * TILE, :], query)
                if j == i:
                    scores = jnp.where(allowed, scores, NEG)
                s_wide[j * TILE : (j + 1) * TILE, :] = scores
                most = jnp.max(scores, axis=0, keepdims=True)
                tops = most if tops is None else jnp.maximum(tops, most)
            top = tops
            total = jnp.zeros((1, TILE), F32)
            for j in range(i + 1):
                there = slice(j * TILE, (j + 1) * TILE)
                weights = jnp.exp(s_wide[there, :] - top)
                total += jnp.sum(weights, axis=0, keepdims=True)
                p_low[there, :] = weights.astype(BF16)
            mixed = dot(v_t[hs, : (i + 1) * TILE], p_low[: (i + 1) * TILE, :])
            out_t[hs, here] = mixed / total
            lse[h, :, here] = top + jnp.log(total)
        return unused

    lax.fori_loop(0, heads, one_head, 0)
    for b in range(blocks):
        here = slice(b * TILE, (b + 1) * TILE)
        o_nat[here, :] = out_t[:, here].T.astype(BF16)
    for p in range(pieces):
        first = pl.multiple_of(scalars[seq * pieces + p], rows)
        part = o_nat[p * rows : (p + 1) * rows, :]
        attn[pl.ds(first, rows), :] = part
        out[pl.ds(first, rows), :] = dot(part, merge[...]).astype(BF16)
    size = out.shape[0] // 4
    for j in range(4):
        outs[j][...] = out[j * size : (j + 1) * size, :]


def attend(scalars, token_parts, packed_parts, shard, width, seqs, pieces):
    total = sum(p.shape[0] for p in token_parts)
    model = token_parts[0].shape[1]
    owners = sum(p.shape[0] for p in packed_parts)
    heads = width // HEAD_DIM
    length = total // seqs
    nat = jax.ShapeDtypeStruct((seqs, length, width), BF16)
    nat_spec = pl.BlockSpec((None, length, width), lambda s, t: (s, 0, 0))
    pairs = heads * length * (length + TILE) // 2 * seqs
    whole = lambda *shape: pl.BlockSpec(shape, lambda s, t: (0,) * len(shape))
    return pl.pallas_call(
        functools.partial(
            attend_kernel, (pieces, heads, shard, model, len(token_parts), len(packed_parts))
        ),
        grid_spec=pltpu.PrefetchScalarGridSpec(
            num_scalar_prefetch=1,
            grid=(seqs,),
            in_specs=[whole(*p.shape) for p in token_parts + packed_parts],
            out_specs=[
                whole(total, model),
                whole(16, model),
                whole(3 * width, model),
                whole(model, width),
                nat_spec,
                nat_spec,
                nat_spec,
                pl.BlockSpec((None, width, length), lambda s, t: (s, 0, 0)),
                pl.BlockSpec((None, heads, 1, length), lambda s, t: (s, 0, 0, 0)),
                whole(total, width),
            ]
            + [whole(total // 4, model)] * 4,
            scratch_shapes=[
                pltpu.VMEM((width, length), BF16),
                pltpu.VMEM((width, length), BF16),
                pltpu.VMEM((heads, length, HEAD_DIM), BF16),
                pltpu.VMEM((length, width), BF16),
                pltpu.VMEM((total, model), BF16),
                pltpu.VMEM((owners,) + packed_parts[0].shape[1:], BF16),
                pltpu.VMEM((model, 4 * width), F32),
                pltpu.VMEM((model, 3 * width), BF16),
                pltpu.VMEM((width, model), BF16),
                pltpu.VMEM((total, model), BF16),
                pltpu.VMEM((length, TILE), F32),
                pltpu.VMEM((length, TILE), BF16),
            ],
        ),
        out_shape=[
            jax.ShapeDtypeStruct((total, model), BF16),
            jax.ShapeDtypeStruct((16, model), F32),
            jax.ShapeDtypeStruct((3 * width, model), BF16),
            jax.ShapeDtypeStruct((model, width), BF16),
            nat,
            nat,
            nat,
            jax.ShapeDtypeStruct((seqs, width, length), F32),
            jax.ShapeDtypeStruct((seqs, heads, 1, length), F32),
            jax.ShapeDtypeStruct((total, width), BF16),
        ]
        + [jax.ShapeDtypeStruct((total // 4, model), BF16)] * 4,
        compiler_params=pltpu.CompilerParams(vmem_limit_bytes=58 * 2**20),
        cost_estimate=pl.CostEstimate(
            flops=32 * HEAD_DIM * pairs, bytes_accessed=24 * total * model, transcendentals=pairs
        ),
        name="attend",
    )(scalars, *token_parts, *packed_parts)


def attend_back_kernel(dims, starts, *refs):
    pieces, heads, shard, ctx, t_index = dims
    row_parts, refs = refs[:4], refs[4:]
    merge_t, heads_t, norm_one, attn, q_pos, k_pos, v_pos, out_t, lse = refs[:9]
    vectors, resid_sums = refs[9:11]
    up_sums, backs, weights = refs[11:15], refs[15:19], refs[19]
    grad_rows, do_nat, q_t, k_t, do_t, q_h, k_h, v_h, do_h, row_dot, dq_t, dk_h, dv_h, g_nat = (
        refs[20:34]
    )
    g_t, back, w_full, p_low, s_low = refs[34:]
    t_pos = starts[t_index]
    seq = pl.program_id(0)
    length, width = q_pos.shape
    model = norm_one.shape[1]
    rows = length // pieces
    blocks = length // TILE
    place = 0
    for part in row_parts:
        grad_rows[place : place + part.shape[0], :] = part[...]
        place += part.shape[0]
    for p in range(pieces):
        first = pl.multiple_of(starts[seq * pieces + p], rows)
        part = dot(grad_rows[pl.ds(first, rows), :], merge_t[...])
        do_nat[p * rows : (p + 1) * rows, :] = part.astype(BF16)
    for b in range(blocks):
        here = slice(b * TILE, (b + 1) * TILE)
        query, key, value, grad = q_pos[here, :], k_pos[here, :], v_pos[here, :], do_nat[here, :]
        q_t[:, here] = query.T
        k_t[:, here] = key.T
        grad_t = grad.T
        do_t[:, here] = grad_t
        product = grad_t.astype(F32) * out_t[:, here]
        for h in range(heads):
            cols = slice(h * HEAD_DIM, (h + 1) * HEAD_DIM)
            q_h[h, here, :] = query[:, cols]
            k_h[h, here, :] = key[:, cols]
            v_h[h, here, :] = value[:, cols]
            do_h[h, here, :] = grad[:, cols]
            row_dot[h, :, here] = jnp.sum(product[cols, :], axis=0, keepdims=True)
    allowed = causal_tile(TILE)

    def one_head(h, unused):
        hs = pl.ds(pl.multiple_of(h * HEAD_DIM, HEAD_DIM), HEAD_DIM)
        for j in range(blocks):
            here = slice(j * TILE, (j + 1) * TILE)
            key, value = k_h[h, here, :], v_h[h, here, :]
            key_t = k_t[hs, here]
            for i in range(j, blocks):
                cols = slice(i * TILE, (i + 1) * TILE)
                scores = dot(key, q_t[hs, cols])
                if i == j:
                    scores = jnp.where(allowed, scores, NEG)
                probs = jnp.exp(scores - lse[h, :, cols])
                slope = probs * (dot(value, do_t[hs, cols]) - row_dot[h, :, cols])
                p_low[:, cols] = probs.astype(BF16)
                s_low[:, cols] = slope.astype(BF16)
            later = slice(j * TILE, length)
            grad_v = dot(p_low[:, later], do_h[h, later, :])
            grad_k = dot(s_low[:, later], q_h[h, later, :])
            add = dot(key_t, s_low[:, later])
            dq_t[hs, later] = add if j == 0 else dq_t[hs, later] + add
            dk_h[h, here, :] = grad_k
            dv_h[h, here, :] = grad_v
        return unused

    lax.fori_loop(0, heads, one_head, 0)
    wide = jnp.zeros((1, 3 * width), F32)
    for b in range(blocks):
        here = slice(b * TILE, (b + 1) * TILE)
        grad_q = dq_t[:, here].T * (HEAD_DIM ** (-0.5))
        grad_k = jnp.concatenate([dk_h[h, here, :] for h in range(heads)], axis=1)
        grad_v = jnp.concatenate([dv_h[h, here, :] for h in range(heads)], axis=1)
        grads = jnp.concatenate([grad_q, grad_k, grad_v], axis=1)
        wide += jnp.sum(grads, axis=0, keepdims=True)
        g_nat[here, :] = grads.astype(BF16)
    w_t = jnp.zeros((3 * width, model), F32)
    m_t = jnp.zeros((width, model), F32)
    column = jnp.zeros((3 * width, 1), F32)
    for p in range(pieces):
        first = pl.multiple_of(starts[seq * pieces + p], rows)
        part = g_nat[p * rows : (p + 1) * rows, :]
        back[pl.ds(first, rows), :] = dot(part, heads_t[...]).astype(BF16)
    for p in range(pieces):
        first = pl.multiple_of(starts[seq * pieces + p], rows)
        g_t[:, :] = g_nat[p * rows : (p + 1) * rows, :].astype(F32).T
        turned = g_t[...]
        column += jnp.sum(turned, axis=1, keepdims=True)
        w_t += dot(turned.astype(BF16), norm_one[pl.ds(first, rows), :])
        mine = attn[pl.ds(first, rows), :].astype(F32).T.astype(BF16)
        m_t += dot(mine, grad_rows[pl.ds(first, rows), :])
    w_full[:, : 3 * width] = w_t.T
    w_full[:, 3 * width :] = m_t.T
    size = back.shape[0] // 4
    for j in range(4):
        backs[j][...] = back[j * size : (j + 1) * size, :]
    factor = heads_t[...].astype(F32)
    group = lax.broadcasted_iota(jnp.int32, (1, model), 1) // width
    spread = lambda part: jnp.where(
        group == t_pos, jnp.concatenate([part] * (model // width), axis=1), 0.0
    )
    shift_sum = jnp.sum(factor * column, axis=0, keepdims=True)
    gain_sum = jnp.sum(factor * w_t, axis=0, keepdims=True) - vectors[1:2, :] * shift_sum
    up_sum = up_sums[0][...] + up_sums[1][...] + up_sums[2][...] + up_sums[3][...]
    lines = jnp.concatenate(
        [
            gain_sum / vectors[0:1, :],
            shift_sum,
            spread(wide[:, :width]),
            spread(wide[:, 2 * width :]),
            resid_sums[0:4, :],
        ],
        axis=0,
    )
    owners = model // shard
    long = model // width * shard
    for i in range(owners):
        k, lane = i * long // model, i * long % model
        here = slice(i * shard, (i + 1) * shard)
        block = [
            w_full[here, :],
            jnp.concatenate([lines[:, here], jnp.zeros((8, model - shard), F32)], axis=1),
            jnp.concatenate(
                [
                    jnp.where(t_pos == k, up_sum[:, lane : lane + long], 0.0),
                    jnp.zeros((1, model - long), F32),
                ],
                axis=1,
            ),
            jnp.zeros((7, model), F32),
        ]
        weights[i % ctx, i // ctx] = jnp.concatenate(block, axis=0).astype(BF16)


def attend_back(starts, row_parts, merge_t, heads_t, norm_one, attn, kept, lines, shard, ctx, pieces):
    q_pos, k_pos, v_pos, out_t, lse = kept
    total, model = norm_one.shape
    width = merge_t.shape[1]
    seqs, length, unused = q_pos.shape
    heads = width // HEAD_DIM
    nat_spec = pl.BlockSpec((None, length, width), lambda s, t: (s, 0, 0))
    whole = lambda *shape: pl.BlockSpec(shape, lambda s, t: (0,) * len(shape))
    pairs = heads * length * (length + TILE) // 2 * seqs
    per_head = pltpu.VMEM((heads, length, HEAD_DIM), BF16)
    by_owner = (ctx, model // shard // ctx, shard + 16, 4 * width)
    across = pltpu.VMEM((width, length), BF16)
    return pl.pallas_call(
        functools.partial(
            attend_back_kernel, (pieces, heads, shard, ctx, starts.shape[0] - 1)
        ),
        grid_spec=pltpu.PrefetchScalarGridSpec(
            num_scalar_prefetch=1,
            grid=(seqs,),
            in_specs=[whole(*p.shape) for p in row_parts]
            + [
                whole(model, width),
                whole(3 * width, model),
                whole(total, model),
                whole(total, width),
                nat_spec,
                nat_spec,
                nat_spec,
                pl.BlockSpec((None, width, length), lambda s, t: (s, 0, 0)),
                pl.BlockSpec((None, heads, 1, length), lambda s, t: (s, 0, 0, 0)),
            ]
            + [whole(*v.shape) for v in lines],
            out_specs=[whole(total // 4, model)] * 4
            + [
                pl.BlockSpec((None,) + by_owner, lambda s, t: (s, 0, 0, 0, 0)),
            ],
            scratch_shapes=[
                pltpu.VMEM((total, model), BF16),
                pltpu.VMEM((length, width), BF16),
                across,
                across,
                across,
                per_head,
                per_head,
                per_head,
                per_head,
                pltpu.VMEM((heads, 1, length), F32),
                pltpu.VMEM((width, length), F32),
                pltpu.VMEM((heads, length, HEAD_DIM), F32),
                pltpu.VMEM((heads, length, HEAD_DIM), F32),
                pltpu.VMEM((length, 3 * width), BF16),
                pltpu.VMEM((3 * width, length // pieces), F32),
                pltpu.VMEM((total, model), BF16),
                pltpu.VMEM((model, 4 * width), F32),
                pltpu.VMEM((TILE, length), BF16),
                pltpu.VMEM((TILE, length), BF16),
            ],
        ),
        out_shape=[jax.ShapeDtypeStruct((total // 4, model), BF16)] * 4
        + [
            jax.ShapeDtypeStruct((seqs,) + by_owner, BF16),
        ],
        compiler_params=pltpu.CompilerParams(vmem_limit_bytes=60 * 2**20),
        cost_estimate=pl.CostEstimate(
            flops=60 * HEAD_DIM * pairs, bytes_accessed=24 * total * model, transcendentals=pairs
        ),
        name="attend_back",
    )(starts, *row_parts, merge_t, heads_t, norm_one, attn, q_pos, k_pos, v_pos, out_t, lse, *lines)


def feed_kernel(
    seqs,
    ctx,
    table,
    norm,
    g_own,
    g_far,
    up,
    down_t,
    bias,
    act,
    pre_low,
    back,
    g_out,
    sums,
):
    step = pl.program_id(0)
    distance = lax.rem(lax.div(step, seqs), ctx)
    grad = jnp.where(distance == 0, g_own[...], g_far[...])
    g_out[...] = grad
    pre = dot(norm[...], up[...]) + bias[...]
    grad_act = dot(grad, down_t[...])
    square = pre * pre
    tangent = jnp.tanh(GELU_C * (pre + 0.044715 * square * pre))
    half = 0.5 * (1.0 + tangent)
    low_act = (pre * half).astype(BF16)
    act[...] = low_act
    slope = half + 0.5 * pre * (1.0 - tangent * tangent) * (
        GELU_C + (GELU_C * 3.0 * 0.044715) * square
    )
    grad_pre = grad_act * slope
    total = jnp.sum(grad_pre, axis=0, keepdims=True)
    sums[...] = jnp.where(step == 0, total, sums[...] + total)
    low = grad_pre.astype(BF16)
    pre_low[...] = low
    back[...] = dot(low, up[...], ((1,), (1,))).astype(BF16)


def feed(table, norm, g_own, g_far, second, bias, seqs, ctx, limit):
    total, model = norm.shape
    rows = g_own.shape[1]
    hidden = second.shape[1] // 2
    steps = total // rows
    by_rows = lambda size: pl.BlockSpec((rows, size), lambda i, t: (i, 0))
    return pl.pallas_call(
        functools.partial(feed_kernel, seqs, ctx),
        grid_spec=pltpu.PrefetchScalarGridSpec(
            num_scalar_prefetch=1,
            grid=(steps,),
            in_specs=[
                by_rows(model),
                pl.BlockSpec((None, rows, model), lambda i, t: (t[i], 0, 0)),
                pl.BlockSpec((None, rows, model), lambda i, t: (t[steps + i], 0, 0)),
                pl.BlockSpec((model, hidden), lambda i, t: (0, 0)),
                pl.BlockSpec((model, hidden), lambda i, t: (0, 1)),
                pl.BlockSpec((1, hidden), lambda i, t: (0, 0)),
            ],
            out_specs=[
                by_rows(hidden),
                by_rows(hidden),
                by_rows(model),
                by_rows(model),
                pl.BlockSpec((1, hidden), lambda i, t: (0, 0)),
            ],
        ),
        out_shape=[
            jax.ShapeDtypeStruct((total, hidden), BF16),
            jax.ShapeDtypeStruct((total, hidden), BF16),
            jax.ShapeDtypeStruct((total, model), BF16),
            jax.ShapeDtypeStruct((total, model), BF16),
            jax.ShapeDtypeStruct((1, hidden), F32),
        ],
        compiler_params=pltpu.CompilerParams(vmem_limit_bytes=limit * 2**20),
        cost_estimate=pl.CostEstimate(
            flops=6 * total * model * hidden,
            bytes_accessed=14 * total * model,
            transcendentals=total * hidden,
        ),
        name="feed",
    )(table, norm, g_own, g_far, second, second, bias)


def resid_kernel(own, beside, across, resid, grad, vectors, out, low, sums):
    step = pl.program_id(0)
    normed, inv_std = layer_stats(resid[...])
    back = own[...].astype(F32) + beside[...].astype(F32) + across[...].astype(F32)
    given = grad[...].astype(F32)
    total = given + norm_back(back, normed, inv_std, vectors[5:6, :])
    out[...] = total
    low[...] = total.astype(BF16)
    add = lambda rows: jnp.sum(rows, axis=0, keepdims=True)
    lines = jnp.concatenate(
        [add(total), add(back * normed), add(back), add(given), jnp.zeros((4, total.shape[1]), F32)],
        axis=0,
    )
    sums[...] = jnp.where(step == 0, lines, sums[...] + lines)


def first_kernel(own, beside, across, rows, grad, vectors, out, low):
    normed, inv_std = layer_stats(rows[...].astype(F32))
    back = own[...].astype(F32) + beside[...].astype(F32) + across[...].astype(F32)
    total = grad[...] + norm_back(back, normed, inv_std, vectors[0:1, :])
    out[...] = total
    low[...] = total.astype(BF16)


def row_wise(kernel, parts, vectors, with_sums):
    total, model = parts[3].shape
    steps = 1
    by_rows = pl.BlockSpec((total // steps, model), lambda i: (i, 0))
    fixed = lambda rows: pl.BlockSpec((rows, model), lambda i: (0, 0))
    return pl.pallas_call(
        kernel,
        grid=(steps,),
        in_specs=[by_rows] * len(parts) + [fixed(16)],
        out_specs=[by_rows, by_rows] + [fixed(8)] * with_sums,
        out_shape=[
            jax.ShapeDtypeStruct((total, model), F32),
            jax.ShapeDtypeStruct((total, model), BF16),
        ]
        + [jax.ShapeDtypeStruct((8, model), F32)] * with_sums,
        cost_estimate=pl.CostEstimate(
            flops=20 * total * model, bytes_accessed=18 * total * model, transcendentals=total
        ),
        compiler_params=pltpu.CompilerParams(vmem_limit_bytes=40 * 2**20),
        name="row_wise",
    )(*parts, vectors)


def pack_kernel(heads, merge, small, up_line, out):
    shard = heads.shape[1]
    model = out.shape[1]
    long = up_line.shape[1]
    top = jnp.concatenate(
        [heads[m].astype(F32) for m in range(3)] + [merge[...].astype(F32).T], axis=1
    )
    gap = lambda size: jnp.zeros((16, size), F32)
    low = [small[...].astype(F32), gap(model // 2 - shard), up_line[...].astype(F32)]
    if model // 2 > long:
        low.append(gap(model // 2 - long))
    out[...] = jnp.concatenate([top, jnp.concatenate(low, axis=1)], axis=0).astype(BF16)


def pack(heads, merge, small, up_line):
    shard, width = heads.shape[1:]
    return pl.pallas_call(
        pack_kernel,
        out_shape=jax.ShapeDtypeStruct((shard + 16, 4 * width), BF16),
        compiler_params=pltpu.CompilerParams(vmem_limit_bytes=16 * 2**20),
        name="pack",
    )(heads, merge, small, up_line)


def heads_kernel(width, a, b, c, d, heads, merge, small):
    shard = merge.shape[1]
    total = sum(part[...].astype(F32) for part in (a, b, c, d))
    for m in range(3):
        heads[m] = total[:shard, m * width : (m + 1) * width]
    merge[...] = total[:shard, 3 * width :].T
    small[...] = total[shard:, :]


def finish_heads(parts, width):
    shard = parts[0].shape[0] - 16
    if len(parts) != 4:
        low = [sum(p.astype(F32) for p in parts)] + [jnp.zeros(parts[0].shape, F32)] * 3
        parts = low
    return pl.pallas_call(
        functools.partial(heads_kernel, width),
        out_shape=[
            jax.ShapeDtypeStruct((3, shard, width), F32),
            jax.ShapeDtypeStruct((width, shard), F32),
            jax.ShapeDtypeStruct((16, 4 * width), F32),
        ],
        name="finish_heads",
    )(*parts)


def swap_tensor(block, bit):
    size = lax.axis_size("tensor")
    return lax.ppermute(block, "tensor", [(i, i ^ bit) for i in range(size)])


def rotate(block, axis, distance):
    size = lax.axis_size(axis)
    return lax.ppermute(block, axis, [(i, (i + distance) % size) for i in range(size)])


def scatter_tensor(parts):
    far = swap_tensor(parts[3], 1)
    near = (parts[2].astype(F32) + far.astype(F32)).astype(BF16)
    across = swap_tensor(near, 2)
    beside = swap_tensor(parts[1], 1)
    return (parts[0], beside, across)


def quarters(rows):
    size = rows.shape[0] // 4
    return [rows[j * size : (j + 1) * size] for j in range(4)]


def add_all(parts):
    return sum(p.astype(F32) for p in parts)


def pick(array, index):
    return lax.dynamic_index_in_dim(array, index, 0, keepdims=False)


def scatter_ctx(blocks):
    ctx, ctx_pos = lax.axis_size("ctx"), lax.axis_index("ctx")
    take = lambda c: lax.dynamic_index_in_dim(blocks, c, 1, keepdims=False)
    total = take(ctx_pos).astype(F32)
    for d in range(1, ctx):
        total += rotate(take((ctx_pos + d) % ctx), "ctx", d).astype(F32)
    return total.astype(BF16)


def scatter_dp(blocks, before_last=None):
    dp, dp_pos = lax.axis_size("dp"), lax.axis_index("dp")
    parts = [pick(blocks, (dp_pos + d) % dp) for d in range(dp)]
    if before_last is not None:
        parts[-1], unused = lax.optimization_barrier((parts[-1], before_last))
    return parts[:1] + [rotate(parts[d], "dp", d) for d in range(1, dp)]


def local(
    tokens,
    cotangent,
    stretch_order,
    attn_gain,
    attn_shift,
    heads_weight,
    heads_bias,
    merge_weight,
    merge_bias,
    feed_gain,
    feed_shift,
    up_weight,
    up_bias,
    down_weight,
    down_bias,
):
    t_size, t_pos = lax.axis_size("tensor"), lax.axis_index("tensor")
    c_size, c_pos = lax.axis_size("ctx"), lax.axis_index("ctx")
    dp_size, dp_pos = lax.axis_size("dp"), lax.axis_index("dp")
    owners = dp_size * c_size
    seqs_in, rows, model = tokens.shape
    seqs = seqs_in // c_size
    shard = heads_weight.shape[1]
    width = heads_weight.shape[2]
    hidden = up_weight.shape[1]
    hidden_all = hidden * t_size
    pieces = c_size * t_size
    span_rows = c_size * seqs * rows

    by_owner = tokens.reshape(c_size, seqs, rows, model)
    near = pick(by_owner, c_pos).reshape(-1, model)
    far = [rotate(pick(by_owner, (c_pos - d) % c_size), "ctx", -d) for d in range(1, c_size)]
    far = jnp.concatenate(far, axis=0).reshape(-1, model)
    near_x = swap_tensor(near, 2)
    far_x = swap_tensor(far, 2)
    own_rows = jnp.concatenate([near, far], axis=0)

    line = lax.broadcasted_iota(jnp.int32, (16, shard), 0)
    small = jnp.zeros((16, shard), BF16)
    for index, vector in enumerate(
        [
            attn_gain[None],
            attn_shift[None],
            heads_bias[0:1],
            heads_bias[1:2],
            merge_bias[None],
            feed_gain[None],
            feed_shift[None],
            down_bias[None],
        ]
    ):
        small = jnp.where(line == index, vector, small)
    up_size = up_bias.shape[0]
    up_line = jnp.where(
        lax.broadcasted_iota(jnp.int32, (16, up_size), 0) == 8, up_bias[None], jnp.zeros((), BF16)
    )
    first_pack = pack(heads_weight, merge_weight, small, up_line)
    by_dp = [first_pack] + [rotate(first_pack, "dp", -d) for d in range(1, dp_size)]
    packed_parts = by_dp + [rotate(p, "ctx", -d) for d in range(1, c_size) for p in by_dp]
    second_pack = jnp.concatenate([up_weight, down_weight.T], axis=1)
    second_pack, by_dp[-1] = lax.optimization_barrier((second_pack, by_dp[-1]))
    packed_parts = [p[None] for p in packed_parts]
    second_all = lax.all_gather(second_pack, ("dp", "ctx"), axis=0, tiled=True)

    near_1, far_1 = swap_tensor(near, 1), swap_tensor(far, 1)
    near_3, far_3 = swap_tensor(near_x, 1), swap_tensor(far_x, 1)
    token_parts = [near, far, near_1, far_1, near_x, far_x, near_3, far_3]

    per_stretch = t_size // 2
    order = lax.dynamic_slice_in_dim(stretch_order, c_pos * seqs, seqs, 0)
    stretches = order.shape[1]
    span = jnp.arange(stretches, dtype=jnp.int32)
    inverse = jnp.sum(
        jnp.where(order[:, :, None] == span[None, None, :], span[None, :, None], 0), axis=1
    )
    stored = inverse[:, :, None]
    part = jnp.arange(per_stretch, dtype=jnp.int32)[None, None, :]
    slot = ((stored % 2) * per_stretch + part) ^ t_pos
    away = (stored // 2 - c_pos) % c_size
    seq_id = jnp.arange(seqs, dtype=jnp.int32)[:, None, None]
    starts = (((slot * c_size + away) * seqs + seq_id) * rows).reshape(-1)
    owner = jnp.arange(owners, dtype=jnp.int32)
    slots = ((owner % c_size - c_pos) % c_size) * dp_size + (owner // c_size - dp_pos) % dp_size
    scalars = jnp.concatenate([starts, slots, t_pos[None].astype(jnp.int32)])

    g_blocks = cotangent.reshape(c_size, seqs, 2, t_size // 2, rows, model)
    bit = t_pos % 2
    g_moved = [
        rotate(
            lax.dynamic_index_in_dim(pick(g_blocks, (c_pos - d) % c_size), bit, 1, keepdims=False),
            "ctx",
            -d,
        )
        for d in range(1, c_size)
    ]
    g_moved = jnp.stack(g_moved)

    norm_one, vec, heads_t, merge_t, q_pos, k_pos, v_pos, out_t, lse, attn, *shares = attend(
        scalars, token_parts, packed_parts, shard, width, seqs, pieces
    )
    shares[3], g_moved = lax.optimization_barrier((shares[3], g_moved))
    merged = add_all(scatter_tensor(shares))
    b_merge, gain_two, shift_two, b_down = vec[4], vec[5], vec[6], vec[7]
    rows_in = own_rows.astype(F32)
    resid = rows_in + merged + b_merge

    normed_two, inv_two = layer_stats(resid)
    norm_0 = (normed_two * gain_two + shift_two).astype(BF16)
    norm_2 = swap_tensor(norm_0, 2)
    norm_1 = swap_tensor(norm_0, 1)
    g_own = cotangent.reshape(-1, rows, model)
    g_far = jnp.stack([g_moved, swap_tensor(g_moved, 1)], axis=2).reshape(-1, rows, model)
    b_up = vec[8:9, :hidden]

    def feed_part(offsets, norm, limit):
        own_table, far_table = [], []
        for j in offsets:
            piece = t_pos ^ j
            for d in range(c_size):
                for q in range(seqs):
                    own_table.append((c_pos * seqs + q) * t_size + piece if d == 0 else 0 * piece)
                    place = (piece // 2) ^ bit
                    far_row = (((d - 1) * seqs + q) * 2 + place) * (t_size // 2) + piece % 2
                    far_table.append(far_row if d > 0 else 0 * piece)
        table = jnp.stack(own_table + far_table).astype(jnp.int32)
        return feed(table, norm, g_own, g_far, second_all, b_up, seqs, c_size, limit)

    act_0, pre_0, back_0, g_0, up_sum_0 = feed_part((0,), norm_0, 60)
    act_1, pre_1, back_1, g_1, up_sum_1 = feed_part((1,), norm_1, 60)
    norm_2, up_sum_0, up_sum_1 = lax.optimization_barrier((norm_2, up_sum_0, up_sum_1))
    norm_3 = swap_tensor(norm_2, 1)
    act_3, pre_3, back_3, g_3, up_sum_3 = feed_part((3,), norm_3, 20)
    act_2, pre_2, back_2, g_2, up_sum_2 = feed_part((2,), norm_2, 20)
    unused, beside, across = scatter_tensor([back_0, back_1, back_2, back_3])

    together = lambda *parts: jnp.concatenate(parts, axis=0)
    norm_all = together(norm_0, norm_1, norm_2, norm_3)
    grad_all = together(g_0, g_1, g_2, g_3)
    grad_down_t = dot(grad_all, together(act_0, act_1, act_2, act_3), ((0,), (0,)))
    grad_up = dot(norm_all, together(pre_0, pre_1, pre_2, pre_3), ((0,), (0,)))
    by_place = lambda grad: grad.astype(BF16).reshape(dp_size, c_size, shard, hidden)
    grad_down_t, grad_up = by_place(grad_down_t), by_place(grad_up)
    down_half = scatter_ctx(grad_down_t)
    across, down_half, grad_up = lax.optimization_barrier((across, down_half, grad_up))
    feed_half = jnp.stack([scatter_ctx(grad_up), down_half], axis=1)
    grad_resid, resid_0, resid_sums = row_wise(
        resid_kernel, [back_0, beside, across, resid, g_0], vec, True
    )
    resid_2 = swap_tensor(resid_0, 2)
    resid_1 = swap_tensor(resid_0, 1)
    w_down = second_all[:, hidden:].T
    mix_0, mix_1, mix_2, mix_3 = (
        dot(a, w_down).astype(BF16) for a in (act_0, act_1, act_2, act_3)
    )
    mix_near = (mix_2.astype(F32) + swap_tensor(mix_3, 1).astype(F32)).astype(BF16)
    resid_2, mix_near, mix_0, mix_1, unused = lax.optimization_barrier(
        (resid_2, mix_near, mix_0, mix_1, feed_half[0, 0, :8, :128])
    )
    mix_across = swap_tensor(mix_near, 2)
    feed_own = lax.psum_scatter(feed_half, "dp", scatter_dimension=0, tiled=False)

    *backs, weights = attend_back(
        scalars,
        [resid_0, resid_1, resid_2, swap_tensor(resid_2, 1)],
        merge_t,
        heads_t,
        norm_one,
        attn,
        (q_pos, k_pos, v_pos, out_t, lse),
        [vec, resid_sums, up_sum_0, up_sum_1, up_sum_2, up_sum_3],
        shard,
        c_size,
        pieces,
    )
    weights, feed_own, mix_across, mix_1, backs[1], backs[3] = lax.optimization_barrier(
        (weights, feed_own, mix_across, mix_1, backs[1], backs[3])
    )
    mix_beside = swap_tensor(mix_1, 1)
    near = (backs[2].astype(F32) + swap_tensor(backs[3], 1).astype(F32)).astype(BF16)
    weights, near = lax.optimization_barrier((weights, near))
    across, beside = swap_tensor(near, 2), swap_tensor(backs[1], 1)
    if seqs == 1:
        weights = weights[0]
    else:
        weights = jnp.sum(weights.astype(F32), axis=0).astype(BF16)
    heads_half = pick(weights, c_pos).astype(F32)
    for d in range(1, c_size):
        heads_half += rotate(pick(weights, (c_pos + d) % c_size), "ctx", d).astype(F32)
    heads_half = heads_ctx = heads_half.astype(BF16)
    heads_parts = scatter_dp(heads_half, across)
    feed_own, unused = lax.optimization_barrier((feed_own, across))
    feed_own = feed_own.astype(F32)
    up_own, down_own = feed_own[0], feed_own[1]
    mixed = add_all([mix_0, mix_beside, mix_across])
    block_rows = (resid + mixed + b_down).astype(BF16)

    def send_back(low, own):
        parts = low.reshape(c_size, seqs, rows, model)
        held = jnp.stack(
            [own.reshape(c_size, seqs, rows, model)[0]]
            + [rotate(parts[d], "ctx", d).astype(own.dtype) for d in range(1, c_size)]
        )
        return jnp.concatenate(
            [pick(held, (c_pos - s) % c_size) for s in range(c_size)], axis=0
        )

    block_rows, unused = lax.optimization_barrier((block_rows, heads_ctx))
    block_out = send_back(block_rows, block_rows)
    tokens_rows, tokens_low = row_wise(
        first_kernel, [backs[0], beside, across, own_rows, grad_resid], vec, False
    )
    tokens_grad = send_back(tokens_low, tokens_rows)
    heads_parts, unused = lax.optimization_barrier((heads_parts, block_out))
    heads_own, merge_own, sums = finish_heads(heads_parts, width)

    sums = add_all([sums] + [rotate(sums, "tensor", d) for d in range(1, t_size)])
    vec_own = sums[:8, :shard]
    up_bias_own = sums[8, : hidden_all // owners]
    return (
        block_out,
        tokens_grad,
        vec_own[0],
        vec_own[1],
        heads_own,
        vec_own[2:4],
        merge_own,
        vec_own[4],
        vec_own[5],
        vec_own[6],
        up_own,
        up_bias_own,
        down_own.T,
        vec_own[7],
    )


def solution(mesh):
    both = P(("dp", "ctx"))
    in_specs = (
        P("dp", ("ctx", "tensor"), None),
        P("dp", "ctx", None),
        P("dp", None),
        both,
        both,
        P(None, ("dp", "ctx"), "tensor"),
        P(None, ("dp", "ctx")),
        P("tensor", ("dp", "ctx")),
        both,
        both,
        both,
        P(("dp", "ctx"), "tensor"),
        both,
        P("tensor", ("dp", "ctx")),
        both,
    )
    out_specs = (
        P("dp", ("ctx", "tensor"), None),
        P("dp", ("ctx", "tensor"), None),
        both,
        both,
        P(None, ("dp", "ctx"), "tensor"),
        P(None, ("dp", "ctx")),
        P("tensor", ("dp", "ctx")),
        both,
        both,
        both,
        P(("dp", "ctx"), "tensor"),
        both,
        P("tensor", ("dp", "ctx")),
        both,
    )
    return jax.shard_map(local, mesh=mesh, in_specs=in_specs, out_specs=out_specs, check_vma=False)
```
